256 devices in a mesh: blk: 32 (over y_hi, z, core), head: 8 (over x, y_lo).
Axes of the slice: x: 4, y: 4 (y_hi: 2, y_lo: 2; y = y_hi * 2 + y_lo), z: 8, core: 2. Of those that a mesh axis runs over, the one named last changes fastest.
Arguments:
- queries: bfloat16 [4096, 32, 128], P('blk', 'head'), may hold values from -6 to 6
- keys: bfloat16 [4096, 32, 128], P('blk', 'head'), may hold values from -6 to 6
- values: bfloat16 [4096, 32, 128], P('blk', 'head'), may hold values from -6 to 6
- outputs: bfloat16 [4096, 32, 128], P('blk', 'head'), may hold values from -4 to 4
- lse: float32 [32, 4096], P('head', 'blk')
- positions: int32 [4096], P('blk'), may hold values from 0 to 4095, as said below
- w_out: bfloat16 [4096, 4096], P('head'), may hold values from -0.09375 to 0.09375
- d_layer: bfloat16 [4096, 4096], P('blk', 'head'), may hold values from -6 to 6
Outputs:
- d_queries: bfloat16 [4096, 32, 128], P('blk', 'head')
- d_keys: bfloat16 [4096, 32, 128], P('blk', 'head')
- d_values: bfloat16 [4096, 32, 128], P('blk', 'head')
The draws below stay inside these ranges and needn't reach their ends.
Inputs may be any that keep to these rules, and one draw needn't show every extreme that they name: A permutation of the positions; each index of blk holds 128 consecutive positions in rising order.
All inputs are finite; a program needn't handle non-finite values.
Results may differ from the reference program's by a relative error of at most 0.006.
Values may be sent and summed in bfloat16 or wider, within the bound.
A program may use at most 128 MiB of HBM per device.

```python
import math
import jax
import jax.numpy as jnp
from jax import lax

D = 4096
HD = 128
TOK_DEV = 128
TOKENS = 4096
HEADS = 32


def block_order(key):
    order = jax.random.permutation(key, TOKENS // TOK_DEV).astype(jnp.int32)
    return (order[:, None] * TOK_DEV + jnp.arange(TOK_DEV, dtype=jnp.int32)[None, :]).reshape(-1)


def draw_positions(key, part):
    return block_order(key)


def draw_lse(key, part):
    placed = block_order(key)
    key = jax.random.fold_in(key, 7)
    offset = jax.random.uniform(key, (HEADS, TOKENS), jnp.float32, -0.5, 0.5)
    return jnp.log(placed.astype(jnp.float32) + 1.0)[None, :] + 0.5 + offset


def shard_levels(key, extent, shards, low, largest):
    def one(dim, shards_of):
        heights = jax.random.uniform(jax.random.fold_in(jax.random.fold_in(key, 6), dim), (shards_of,), jnp.float32, low / len(shards), largest / len(shards))
        return jnp.repeat(jnp.exp(heights), extent[dim] // shards_of).reshape((-1,) + (1,) * (len(extent) - dim - 1))

    level = one(*shards[0])
    for cut in shards[1:]:
        level = level * one(*cut)
    return level


def noise(key, dims, spread, reach, pieces=(), kind=jnp.bfloat16):
    entries = jax.random.normal(key, dims, jnp.float32) * spread
    if len(pieces) > 0:
        entries = shard_levels(key, dims, pieces, -0.22, 0.18) * entries
    return jnp.clip(entries, min=-reach, max=reach).astype(kind)


def setup_inputs(seed: int = 0) -> dict:
    streams_of = jax.random.split(jax.random.key(seed), 9)
    return {
        "queries": noise(streams_of[0], (TOKENS, HEADS, HD), 1.0, 6.0, ((0, 32), (1, 8))),
        "keys": noise(streams_of[1], (TOKENS, HEADS, HD), 1.0, 6.0, ((0, 32), (1, 8))),
        "values": noise(streams_of[2], (TOKENS, HEADS, HD), 1.0, 6.0, ((0, 32), (1, 8))),
        "outputs": noise(streams_of[3], (TOKENS, HEADS, HD), 0.5, 4.0, ((0, 32), (1, 8))),
        "lse": draw_lse(jax.random.fold_in(streams_of[8], 71), 0),
        "positions": draw_positions(jax.random.fold_in(streams_of[8], 71), 0),
        "w_out": noise(streams_of[6], (HEADS * HD, D), (HEADS * HD) ** -0.5, 0.09375, ((0, 8),)),
        "d_layer": noise(streams_of[7], (TOKENS, D), 1.0, 6.0, ((0, 32), (1, 8))),
    }


def head_grads(queries, keys, values, d_attn, lse_row, delta, positions):
    scale = 1.0 / math.sqrt(HD)
    block = math.gcd(TOKENS, 1024)

    def one(d_q, index):
        offset = index * block
        key_blk = lax.dynamic_slice_in_dim(keys, offset, block, 0)
        value_blk = lax.dynamic_slice_in_dim(values, offset, block, 0)
        key_pos = lax.dynamic_slice_in_dim(positions, offset, block, 0)
        scores = jnp.dot(queries, key_blk.T, preferred_element_type=jnp.float32) * scale
        visible = key_pos[None, :] <= positions[:, None]
        probs = jnp.where(visible, jnp.exp(jnp.where(visible, scores - lse_row[:, None], 0.0)), 0.0)
        probs_b = probs.astype(jnp.bfloat16)
        d_v = jnp.dot(probs_b.T, d_attn, preferred_element_type=jnp.float32)
        d_probs = jnp.dot(d_attn, value_blk.T, preferred_element_type=jnp.float32)
        d_scores = (probs * (d_probs - delta[:, None])).astype(jnp.bfloat16)
        d_k = jnp.dot(d_scores.T, queries, preferred_element_type=jnp.float32) * scale
        d_q = d_q + jnp.dot(d_scores, key_blk, preferred_element_type=jnp.float32) * scale
        return (d_q, (d_k.astype(jnp.bfloat16), d_v.astype(jnp.bfloat16)))
    start = jnp.zeros((TOKENS, HD), jnp.float32)
    d_q, (d_k, d_v) = lax.scan(one, start, jnp.arange(TOKENS // block, dtype=jnp.int32))
    return (d_q.astype(jnp.bfloat16), d_k.reshape(TOKENS, HD), d_v.reshape(TOKENS, HD))

def reference(queries, keys, values, outputs, lse, positions, w_out, d_layer):
    d_attn = jnp.dot(d_layer, w_out.T, preferred_element_type=jnp.float32).astype(jnp.bfloat16)
    d_attn = d_attn.reshape(TOKENS, HEADS, HD)
    delta = lax.optimization_barrier(jnp.sum(d_attn.astype(jnp.float32) * outputs.astype(jnp.float32), axis=-1))

    def per_head(items):
        q_h, k_h, v_h, do_h, lse_h, delta_h = items
        return head_grads(q_h, k_h, v_h, do_h, lse_h, delta_h, positions)
    d_q, d_k, d_v = lax.map(per_head, (queries.transpose(1, 0, 2), keys.transpose(1, 0, 2), values.transpose(1, 0, 2), d_attn.transpose(1, 0, 2), lse, delta.T))
    return (d_q.transpose(1, 0, 2), d_k.transpose(1, 0, 2), d_v.transpose(1, 0, 2))
```

```python
import functools
import math

import jax
import jax.numpy as jnp
from jax import lax
from jax.experimental import pallas as pl
from jax.experimental.pallas import tpu as pltpu
from jax.sharding import PartitionSpec as P

MESH = pl.DeviceIdType.MESH
BF = jnp.bfloat16
F32 = jnp.float32
LOG2E = 1.0 / math.log(2.0)
SCALE = 1.0 / math.sqrt(128.0)
KV_ROWS = 272
QA_ROWS = 144
NT = (((1,), (1,)), ((), ()))
TN = (((0,), (0,)), ((), ()))
NN = (((1,), (0,)), ((), ()))


def dot(a, b, dims):
    return lax.dot_general(a, b, dims, preferred_element_type=F32)


def thirds(value):
    high = value.astype(BF)
    rest = value - high.astype(F32)
    middle = rest.astype(BF)
    low = (rest - middle.astype(F32)).astype(BF)
    return high, middle, low


def kernel(
    dl, w_hbm, o_ref, kv_in, qa_in, outq, outkv,
    gath, w_v, kv, qa, late, late_out, dq_acc, dk_acc, dv_acc,
    sq, rq, skv, rkv, fq, fkv, send, recv, local,
):
    b = lax.axis_index("blk")
    hd = lax.axis_index("head")
    yh, z, c = b // 16, (b // 2) % 8, b % 2
    m = z // 2
    sg = 2 * (z % 2) - 1
    x, yl = hd // 2, hd % 2

    def at_z(by):
        return {"blk": yh * 16 + ((z + by + 8) % 8) * 2 + c}

    sibling = {"blk": yh * 16 + z * 2 + (1 - c)}
    across = {"blk": (1 - yh) * 16 + z * 2 + c}
    zpart = at_z(-sg)
    to_z = (None, at_z(sg), at_z(-2 * sg), at_z(3 * sg))
    from_z = (None, at_z(sg), at_z(2 * sg), at_z(3 * sg))
    head_of = (m, (m + sg + 4) % 4, (m - sg + 4) % 4, (m + 2) % 4)
    beside = {"head": x * 2 + (1 - yl)}
    right = {"head": ((x + 1) % 4) * 2 + yl}
    left = {"head": ((x + 3) % 4) * 2 + yl}

    count = [0]
    started = []

    def remote(src, dst, device):
        k = count[0]
        count[0] = k + 1
        return pltpu.make_async_remote_copy(
            src_ref=src, dst_ref=dst, send_sem=send.at[k], recv_sem=recv.at[k],
            device_id=device, device_id_type=MESH,
        )

    def go(copy):
        copy.start()
        started.append(copy)

    w_copies = []
    for r in range(8):
        dx, dy = r // 2, r % 2
        col = (((x + dx) % 4) * 2 + (yl + dy) % 2) * 512
        w_copies.append(
            pltpu.make_async_copy(w_hbm.at[:, pl.ds(pl.multiple_of(col, 512), 512)], w_v.at[r], local.at[r])
        )
    for r in (0, 1, 6, 2, 7, 3, 4, 5):
        w_copies[r].start()
    own_kv = pltpu.make_async_copy(kv_in.at[m], kv.at[0, 0], local.at[8])
    own_qa = pltpu.make_async_copy(qa_in.at[m], qa.at[0, 0], local.at[9])
    own_kv.start()
    own_qa.start()

    barrier = pltpu.get_barrier_semaphore()
    partners = (beside, right, left, sibling, across, zpart, at_z(sg), at_z(-2 * sg), at_z(2 * sg), at_z(3 * sg))
    for device in partners:
        pl.semaphore_signal(barrier, inc=1, device_id=device, device_id_type=MESH)
    pl.semaphore_wait(barrier, len(partners))

    g_side = remote(dl, gath.at[1], beside)
    g_r0 = remote(dl, gath.at[6], right)
    g_l0 = remote(dl, gath.at[2], left)
    go(g_side)
    go(g_r0)
    go(g_l0)
    kv_z = [None] + [remote(kv_in.at[head_of[d]], kv.at[0, d], to_z[d]) for d in (1, 2, 3)]
    qa_z = [None] + [remote(qa_in.at[head_of[d]], qa.at[0, d], to_z[d]) for d in (1, 2, 3)]
    for d in (3, 2, 1):
        go(qa_z[d])
    for d in (3, 2, 1):
        go(kv_z[d])
    g_r1 = remote(gath.at[1], gath.at[7], right)
    g_l1 = remote(gath.at[1], gath.at[3], left)
    g_r2 = remote(gath.at[6, pl.ds(0, 64)], gath.at[4, pl.ds(0, 64)], right)
    g_l2 = remote(gath.at[2, pl.ds(64, 64)], gath.at[4, pl.ds(64, 64)], left)
    g_r3 = remote(gath.at[7, pl.ds(0, 64)], gath.at[5, pl.ds(0, 64)], right)
    g_l3 = remote(gath.at[3, pl.ds(64, 64)], gath.at[5, pl.ds(64, 64)], left)
    qa_sib = [remote(qa.at[0, d], qa.at[1, d], sibling) for d in range(4)]
    qa_zp = [remote(qa.at[0, d], qa.at[2, d], zpart) for d in range(4)]
    qa_fwd = [remote(qa.at[2, d], qa.at[3, d], sibling) for d in range(4)]
    kv_y = [remote(kv.at[0, d], kv.at[1, d], across) for d in range(4)]

    own_qa.wait()
    go(qa_zp[0])
    go(qa_sib[0])
    own_kv.wait()
    go(kv_y[0])

    def project(r):
        w_copies[r].wait()
        shard = dl[...] if r == 0 else gath[r]
        return dot(shard, w_v[r], NT)

    def relay_early(d):
        qa_z[d].wait_recv()
        go(qa_zp[d])
        go(qa_sib[d])
        kv_z[d].wait_recv()
        go(kv_y[d])

    g_side.wait_recv()
    go(g_r1)
    go(g_l1)
    total = project(0)
    g_r0.wait_recv()
    go(g_r2)
    g_l0.wait_recv()
    go(g_l2)
    relay_early(1)
    total += project(1)
    total += project(6)
    g_r1.wait_recv()
    go(g_r3)
    g_l1.wait_recv()
    go(g_l3)
    relay_early(2)
    total += project(2)
    total += project(7)
    relay_early(3)
    total += project(3)
    g_r2.wait_recv()
    g_l2.wait_recv()
    total += project(4)
    g_r3.wait_recv()
    g_l3.wait_recv()
    total += project(5)

    for h in range(4):
        part = total[:, h * 128:(h + 1) * 128].astype(BF)
        late_out[h, pl.ds(0, 128), :] = part
        col = jnp.sum(part.astype(F32) * o_ref[h].astype(F32), axis=1, keepdims=True)
        row = jnp.transpose(jnp.broadcast_to(col, (128, 128)))[0:1, :]
        hi, mid, low = thirds(row)
        rows = [hi.astype(F32), mid.astype(F32), low.astype(F32), jnp.zeros((13, 128), F32)]
        late_out[h, pl.ds(128, 16), :] = jnp.concatenate(rows, axis=0).astype(BF)

    late_z = [None] + [remote(late_out.at[head_of[d]], late.at[0, d], to_z[d]) for d in (1, 2, 3)]
    for d in (3, 2, 1):
        go(late_z[d])
    own_late = pltpu.make_async_copy(late_out.at[m], late.at[0, 0], local.at[10])
    own_late.start()
    late_sib = [remote(late.at[0, d], late.at[1, d], sibling) for d in range(4)]
    late_zp = [remote(late.at[0, d], late.at[2, d], zpart) for d in range(4)]
    late_fwd = [remote(late.at[2, d], late.at[3, d], sibling) for d in range(4)]
    own_late.wait()
    go(late_zp[0])
    go(late_sib[0])
    for d in range(4):
        qa_zp[d].wait_recv()
        go(qa_fwd[d])
    for d in (1, 2, 3):
        late_z[d].wait_recv()
        go(late_zp[d])
        go(late_sib[d])

    def tile(kk, kp, qc, qp, diagonal, first):
        k = jnp.concatenate([kv[kk, 2 * kp + i, pl.ds(128, 128), :] for i in (0, 1)], axis=0)
        v = jnp.concatenate([kv[kk, 2 * kp + i, pl.ds(0, 128), :] for i in (0, 1)], axis=0)
        q = jnp.concatenate([qa[qc, 2 * qp + i, pl.ds(16, 128), :] for i in (0, 1)], axis=0)
        do = jnp.concatenate([late[qc, 2 * qp + i, pl.ds(0, 128), :] for i in (0, 1)], axis=0)
        aux = jnp.concatenate([qa[qc, 2 * qp + i, pl.ds(0, 16), :].astype(F32) for i in (0, 1)], axis=1)
        aux2 = jnp.concatenate([late[qc, 2 * qp + i, pl.ds(128, 16), :].astype(F32) for i in (0, 1)], axis=1)
        q_rank = aux[0:1]
        lse = (aux[1:2] + aux[2:3] + aux[3:4]) * LOG2E
        delta = aux2[0:1] + aux2[1:2] + aux2[2:3]
        scores = dot(k, q, NT)
        d_probs = dot(v, do, NT)
        halves = []
        for i in (0, 1):
            k_rank = kv[kk, 2 * kp + i, pl.ds(256, 16), :].astype(F32)[0:1]
            k_rank = jnp.concatenate([k_rank, k_rank], axis=1)
            shift = jnp.where(k_rank <= q_rank, lse, jnp.inf)
            halves.append(scores[i * 128:(i + 1) * 128] * (SCALE * LOG2E) - shift)
        exponent = jnp.concatenate(halves, axis=0)
        if diagonal:
            row = lax.broadcasted_iota(jnp.int32, (256, 256), 0)
            col = lax.broadcasted_iota(jnp.int32, (256, 256), 1)
            seen = (row <= col) | ((row >= 128) & (col < 128))
            exponent = jnp.where(seen, exponent, -jnp.inf)
        probs = jnp.exp2(exponent)
        probs_b = probs.astype(BF)
        d_scores = (probs * (d_probs - delta)).astype(BF)
        rows = pl.ds(kp * 256, 256)
        d_v = dot(probs_b, do, NN)
        d_k = dot(d_scores, q, NN)
        d_q = dot(d_scores, k, TN)
        if first:
            dv_acc[kk, rows, :] = d_v
            dk_acc[kk, rows, :] = d_k
        else:
            dv_acc[kk, rows, :] += d_v
            dk_acc[kk, rows, :] += d_k
        return d_q

    def sweep(kk, qc, fresh_q, fresh_k):
        def body(qp, carry):
            d_q = tile(kk, 0, qc, qp, False, False)
            d_q += tile(kk, 1, qc, qp, False, False)
            rows = pl.ds(pl.multiple_of(qp * 256, 256), 256)
            if fresh_q:
                dq_acc[qc, rows, :] = d_q
            else:
                dq_acc[qc, rows, :] += d_q
            return carry

        if fresh_k:
            dv_acc[kk] = jnp.zeros((512, 128), F32)
            dk_acc[kk] = jnp.zeros((512, 128), F32)
        lax.fori_loop(0, 2, body, 0)

    for d in range(4):
        kv_y[d].wait_recv()
    sweep(1, 0, True, True)
    for d in range(4):
        late_zp[d].wait_recv()
        go(late_fwd[d])
    for d in range(4):
        qa_sib[d].wait_recv()
        late_sib[d].wait_recv()
    sweep(1, 1, True, False)
    sweep(1, 2, True, False)
    for d in range(4):
        qa_fwd[d].wait_recv()
        late_fwd[d].wait_recv()
    sweep(1, 3, True, False)
    for d in range(4):
        skv[d, pl.ds(0, 128), :] = dv_acc[1, pl.ds(d * 128, 128), :].astype(BF)
        skv[d, pl.ds(128, 128), :] = (dk_acc[1, pl.ds(d * 128, 128), :] * SCALE).astype(BF)
    kv_back = remote(skv, rkv, across)
    go(kv_back)

    sweep(0, 3, False, True)
    sq[0] = (dq_acc[3] * SCALE).astype(BF)
    q_back3 = remote(sq.at[0], rq.at[0], sibling)
    go(q_back3)
    sweep(0, 2, False, False)
    q_back3.wait_recv()
    sq[1] = (dq_acc[2] * SCALE + rq[0].astype(F32)).astype(BF)
    q_back2 = remote(sq.at[1], rq.at[1], zpart)
    go(q_back2)
    sweep(0, 1, False, False)
    sq[2] = (dq_acc[1] * SCALE).astype(BF)
    q_back1 = remote(sq.at[2], rq.at[2], sibling)
    go(q_back1)
    for qp in (0, 1):
        d_q = tile(0, 0, 0, qp, qp == 0, False)
        d_q += tile(0, 1, 0, qp, qp == 1, False)
        dq_acc[0, pl.ds(qp * 256, 256), :] += d_q

    kv_back.wait_recv()
    out_kv = [None] + [remote(fkv.at[d], outkv.at[m], from_z[d]) for d in (1, 2, 3)]
    out_q = [None] + [remote(fq.at[d], outq.at[m], from_z[d]) for d in (1, 2, 3)]
    for d in (3, 2, 1, 0):
        rows = pl.ds(d * 128, 128)
        fkv[d, pl.ds(0, 128), :] = (dv_acc[0, rows, :] + rkv[d, pl.ds(0, 128), :].astype(F32)).astype(BF)
        fkv[d, pl.ds(128, 128), :] = (
            dk_acc[0, rows, :] * SCALE + rkv[d, pl.ds(128, 128), :].astype(F32)
        ).astype(BF)
        if d > 0:
            go(out_kv[d])
    q_back1.wait_recv()
    q_back2.wait_recv()
    for d in (3, 2, 1, 0):
        rows = pl.ds(d * 128, 128)
        fq[d] = (
            dq_acc[0, rows, :] * SCALE + (rq[1, rows, :].astype(F32) + rq[2, rows, :].astype(F32))
        ).astype(BF)
        if d > 0:
            go(out_q[d])
    keep_kv = pltpu.make_async_copy(fkv.at[0], outkv.at[m], local.at[11])
    keep_q = pltpu.make_async_copy(fq.at[0], outq.at[m], local.at[12])
    keep_kv.start()
    keep_q.start()
    keep_kv.wait()
    keep_q.wait()
    for d in (1, 2, 3):
        out_kv[d].wait_recv()
        out_q[d].wait_recv()
    for copy in started:
        copy.wait_send()


COPIES = 80


def on_device(queries, keys, values, outputs, lse, positions, w_out, d_layer):
    rank = jnp.broadcast_to((positions[0] // 128).astype(BF), (4, 128))

    def rounded(a):
        return lax.reduce_precision(a, exponent_bits=8, mantissa_bits=7)

    high = rounded(lse)
    middle = rounded(lse - high)
    low = rounded(lse - high - middle)
    aux = jnp.stack([rank] + [part.astype(BF) for part in (high, middle, low)], axis=1)
    aux = jnp.pad(aux, ((0, 0), (0, 12), (0, 0)))
    q, k, v, o = (jnp.transpose(a, (1, 0, 2)) for a in (queries, keys, values, outputs))
    kv_in = jnp.concatenate([v, k, aux], axis=1)
    qa_in = jnp.concatenate([aux, q], axis=1)
    vmem = pl.BlockSpec(memory_space=pltpu.VMEM)
    out_q, out_kv = pl.pallas_call(
        kernel,
        out_shape=(jax.ShapeDtypeStruct((4, 128, 128), BF), jax.ShapeDtypeStruct((4, 256, 128), BF)),
        in_specs=[vmem, pl.BlockSpec(memory_space=pl.ANY), vmem, vmem, vmem],
        out_specs=(vmem, vmem),
        scratch_shapes=[
            pltpu.VMEM((8, 128, 512), BF),
            pltpu.VMEM((8, 512, 512), BF),
            pltpu.VMEM((2, 4, KV_ROWS, 128), BF),
            pltpu.VMEM((4, 4, QA_ROWS, 128), BF),
            pltpu.VMEM((4, 4, QA_ROWS, 128), BF),
            pltpu.VMEM((4, QA_ROWS, 128), BF),
            pltpu.VMEM((4, 512, 128), F32),
            pltpu.VMEM((2, 512, 128), F32),
            pltpu.VMEM((2, 512, 128), F32),
            pltpu.VMEM((3, 512, 128), BF),
            pltpu.VMEM((3, 512, 128), BF),
            pltpu.VMEM((4, 256, 128), BF),
            pltpu.VMEM((4, 256, 128), BF),
            pltpu.VMEM((4, 128, 128), BF),
            pltpu.VMEM((4, 256, 128), BF),
            pltpu.SemaphoreType.DMA((COPIES,)),
            pltpu.SemaphoreType.DMA((COPIES,)),
            pltpu.SemaphoreType.DMA((16,)),
        ],
        compiler_params=pltpu.CompilerParams(
            collective_id=0, has_side_effects=True, vmem_limit_bytes=48 * 1024 * 1024
        ),
    )(d_layer, w_out, o, kv_in, qa_in)
    d_q = jnp.transpose(out_q, (1, 0, 2))
    d_v = jnp.transpose(out_kv[:, :128], (1, 0, 2))
    d_k = jnp.transpose(out_kv[:, 128:], (1, 0, 2))
    return (d_q, d_k, d_v)


def solution(mesh):
    in_specs = (
        P("blk", "head", None),
        P("blk", "head", None),
        P("blk", "head", None),
        P("blk", "head", None),
        P("head", "blk"),
        P("blk"),
        P("head", None),
        P("blk", "head"),
    )
    out_specs = (P("blk", "head", None), P("blk", "head", None), P("blk", "head", None))
    return jax.shard_map(
        on_device, mesh=mesh, in_specs=in_specs, out_specs=out_specs, check_vma=False
    )
```

```python
import functools
import math

import jax
import jax.numpy as jnp
from jax import lax
from jax.experimental import pallas as pl
from jax.experimental.pallas import tpu as pltpu
from jax.sharding import PartitionSpec as P

MESH = pl.DeviceIdType.MESH
BF = jnp.bfloat16
F32 = jnp.float32
LOG2E = 1.0 / math.log(2.0)
SCALE = 1.0 / math.sqrt(128.0)
KV_ROWS = 272
QA_ROWS = 144
VMEM_BYTES = 63 * 1024 * 1024
NT = (((1,), (1,)), ((), ()))
TN = (((0,), (0,)), ((), ()))
NN = (((1,), (0,)), ((), ()))


def dot(a, b, dims):
    return lax.dot_general(a, b, dims, preferred_element_type=F32)


def thirds(value):
    high = value.astype(BF)
    rest = value - high.astype(F32)
    middle = rest.astype(BF)
    low = (rest - middle.astype(F32)).astype(BF)
    return high, middle, low


def kernel(
    dl, w_hbm, v_hbm, k_hbm, q_hbm, o_hbm, lse_ref, pos_ref, out,
    raw, dl_v, gath, w_v, kv_st, qa_st, kv, qa, late, late_out, k_t, dq_acc, dk_acc, dv_acc,
    sq, rq, skv, rkv, fq, fkv, send, recv, local,
):
    b = lax.axis_index("blk")
    hd = lax.axis_index("head")
    yh, z, c = b // 16, (b // 2) % 8, b % 2
    m = z // 2
    sg = 2 * (z % 2) - 1
    x, yl = hd // 2, hd % 2

    def at_z(by):
        return {"blk": yh * 16 + ((z + by + 8) % 8) * 2 + c}

    sibling = {"blk": yh * 16 + z * 2 + (1 - c)}
    across = {"blk": (1 - yh) * 16 + z * 2 + c}
    zpart = at_z(-sg)
    to_z = (None, at_z(sg), at_z(-2 * sg), at_z(3 * sg))
    from_z = (None, at_z(sg), at_z(2 * sg), at_z(3 * sg))
    head_of = (m, (m + sg + 4) % 4, (m - sg + 4) % 4, (m + 2) % 4)
    beside = {"head": x * 2 + (1 - yl)}
    right = {"head": ((x + 1) % 4) * 2 + yl}
    left = {"head": ((x + 3) % 4) * 2 + yl}

    count = [0]
    started = []

    def remote(src, dst, device):
        k = count[0]
        count[0] = k + 1
        return pltpu.make_async_remote_copy(
            src_ref=src, dst_ref=dst, send_sem=send.at[k], recv_sem=recv.at[k],
            device_id=device, device_id_type=MESH,
        )

    def go(copy):
        copy.start()
        started.append(copy)

    raw_copies = [pltpu.make_async_copy(a, raw.at[i], local.at[8 + i]) for i, a in enumerate((v_hbm, k_hbm, q_hbm, o_hbm))]
    dl_copy = pltpu.make_async_copy(dl, dl_v, local.at[12])
    w_copies = []
    for r in range(8):
        dx, dy = r // 2, r % 2
        col = (((x + dx) % 4) * 2 + (yl + dy) % 2) * 512
        w_copies.append(
            pltpu.make_async_copy(w_hbm.at[:, pl.ds(pl.multiple_of(col, 512), 512)], w_v.at[r], local.at[r])
        )
    for copy in raw_copies[:3] + [dl_copy]:
        copy.start()

    barrier = pltpu.get_barrier_semaphore()
    partners = (beside, right, left, sibling, across, zpart, at_z(sg), at_z(-2 * sg), at_z(2 * sg), at_z(3 * sg))
    for device in partners:
        pl.semaphore_signal(barrier, inc=1, device_id=device, device_id_type=MESH)

    rank = jnp.broadcast_to((pos_ref[...] // 128).astype(F32)[:, 0:1], (1, 128))
    aux = []
    for h in range(4):
        parts = thirds(lse_ref[pl.ds(h, 1), :])
        rows = [rank] + [part.astype(F32) for part in parts] + [jnp.zeros((12, 128), F32)]
        aux.append(jnp.concatenate(rows, axis=0).astype(BF))

    def relay_out(i):
        raw_copies[i].wait()
        return jnp.transpose(raw[i].astype(F32), (1, 0, 2)).astype(BF)

    kv_st[:, pl.ds(0, 128), :] = relay_out(0)
    kv_st[:, pl.ds(128, 128), :] = relay_out(1)
    for h in range(4):
        kv_st[h, pl.ds(256, 16), :] = aux[h]
        qa_st[h, pl.ds(0, 16), :] = aux[h]
    pl.semaphore_wait(barrier, len(partners))

    halves = (pl.ds(0, 64), pl.ds(64, 64))
    g_side = [remote(dl.at[r], gath.at[1, r], beside) for r in halves]
    g_r0 = [remote(dl.at[r], gath.at[6, r], right) for r in halves]
    g_l0 = [remote(dl.at[r], gath.at[2, r], left) for r in halves]
    g_r1 = [remote(gath.at[1, r], gath.at[7, r], right) for r in halves]
    g_l1 = [remote(gath.at[1, r], gath.at[3, r], left) for r in halves]
    g_r2 = remote(gath.at[6, halves[0]], gath.at[4, halves[0]], right)
    g_l2 = remote(gath.at[2, halves[1]], gath.at[4, halves[1]], left)
    g_r3 = remote(gath.at[7, halves[0]], gath.at[5, halves[0]], right)
    g_l3 = remote(gath.at[3, halves[1]], gath.at[5, halves[1]], left)
    for copy in (g_side[0], g_r0[0], g_l0[1], g_side[1], g_r0[1], g_l0[0]):
        go(copy)

    kv_z = [None] + [remote(kv_st.at[head_of[d]], kv.at[0, d], to_z[d]) for d in (1, 2, 3)]
    qa_z = [None] + [remote(qa_st.at[head_of[d]], qa.at[0, d], to_z[d]) for d in (1, 2, 3)]
    qa_sib = [remote(qa_st.at[m] if d == 0 else qa.at[0, d], qa.at[1, d], sibling) for d in range(4)]
    qa_zp = [remote(qa_st.at[m] if d == 0 else qa.at[0, d], qa.at[2, d], zpart) for d in range(4)]
    qa_fwd = [remote(qa.at[2, d], qa.at[3, d], sibling) for d in range(4)]
    kv_y = [remote(kv_st.at[m] if d == 0 else kv.at[0, d], kv.at[1, d], across) for d in range(4)]
    for d in (3, 2, 1):
        go(kv_z[d])
    go(kv_y[0])
    for copy in (raw_copies[3], *(w_copies[r] for r in (0, 1, 6, 2, 7, 3, 4, 5))):
        copy.start()
    qa_st[:, pl.ds(16, 128), :] = relay_out(2)
    for d in (3, 2, 1):
        go(qa_z[d])
    go(qa_zp[0])
    go(qa_sib[0])
    kv[0, 0] = kv_st[m]
    qa[0, 0] = qa_st[m]

    def project(r):
        w_copies[r].wait()
        shard = dl_v[...] if r == 0 else gath[r]
        return dot(shard, w_v[r], NT)

    g_side[0].wait_recv()
    go(g_r1[0])
    go(g_l1[0])
    g_r0[0].wait_recv()
    go(g_r2)
    g_l0[1].wait_recv()
    go(g_l2)
    g_side[1].wait_recv()
    go(g_l1[1])
    go(g_r1[1])
    o_heads = relay_out(3)
    dl_copy.wait()
    total = project(0)
    total += project(1)
    g_r1[0].wait_recv()
    go(g_r3)
    g_l1[1].wait_recv()
    go(g_l3)
    g_r0[1].wait_recv()
    total += project(6)
    g_l0[0].wait_recv()
    total += project(2)
    g_r1[1].wait_recv()
    total += project(7)
    g_l1[0].wait_recv()
    total += project(3)
    for d in (1, 2, 3):
        kv_z[d].wait_recv()
        go(kv_y[d])
        qa_z[d].wait_recv()
        go(qa_zp[d])
        go(qa_sib[d])
    g_r2.wait_recv()
    g_l2.wait_recv()
    total += project(4)
    g_r3.wait_recv()
    g_l3.wait_recv()
    total += project(5)

    for h in range(4):
        part = total[:, h * 128:(h + 1) * 128].astype(BF)
        late_out[h, pl.ds(0, 128), :] = part
        col = jnp.sum(part.astype(F32) * o_heads[h].astype(F32), axis=1, keepdims=True)
        row = jnp.transpose(jnp.broadcast_to(col, (128, 128)))[0:1, :]
        rows = [part.astype(F32) for part in thirds(row)] + [jnp.zeros((13, 128), F32)]
        late_out[h, pl.ds(128, 16), :] = jnp.concatenate(rows, axis=0).astype(BF)

    late_z = [None] + [remote(late_out.at[head_of[d]], late.at[0, d], to_z[d]) for d in (1, 2, 3)]
    late_sib = [remote(late_out.at[m] if d == 0 else late.at[0, d], late.at[1, d], sibling) for d in range(4)]
    late_zp = [remote(late_out.at[m] if d == 0 else late.at[0, d], late.at[2, d], zpart) for d in range(4)]
    late_fwd = [remote(late.at[2, d], late.at[3, d], sibling) for d in range(4)]
    for d in (3, 2, 1):
        go(late_z[d])
    go(late_zp[0])
    go(late_sib[0])
    late[0, 0] = late_out[m]
    for d in range(4):
        qa_zp[d].wait_recv()
        go(qa_fwd[d])
    for d in range(4):
        k_t[0, :, pl.ds(d * 128, 128)] = jnp.transpose(kv[0, d, pl.ds(128, 128), :].astype(F32)).astype(BF)
    for d in range(4):
        kv_y[d].wait_recv()
        k_t[1, :, pl.ds(d * 128, 128)] = jnp.transpose(kv[1, d, pl.ds(128, 128), :].astype(F32)).astype(BF)
    for d in (1, 2, 3):
        late_z[d].wait_recv()
        go(late_zp[d])
        go(late_sib[d])

    def step(kk, kp, qc, first_k=False, first_q=False):
        keys = [kv[kk, 2 * kp + i, pl.ds(128, 128), :] for i in (0, 1)]
        k = jnp.concatenate(keys, axis=0)
        v = jnp.concatenate([kv[kk, 2 * kp + i, pl.ds(0, 128), :] for i in (0, 1)], axis=0)
        q = jnp.concatenate([qa[qc, i, pl.ds(16, 128), :] for i in range(4)], axis=0)
        do = jnp.concatenate([late[qc, i, pl.ds(0, 128), :] for i in range(4)], axis=0)
        aux = jnp.concatenate([qa[qc, i, pl.ds(0, 16), :].astype(F32) for i in range(4)], axis=1)
        aux2 = jnp.concatenate([late[qc, i, pl.ds(128, 16), :].astype(F32) for i in range(4)], axis=1)
        q_rank = aux[0:1]
        lse = (aux[1:2] + aux[2:3] + aux[3:4]) * LOG2E
        delta = aux2[0:1] + aux2[1:2] + aux2[2:3]
        scores = dot(k, q, NT)
        d_probs = dot(v, do, NT)
        parts = []
        for i in (0, 1):
            k_rank = kv[kk, 2 * kp + i, pl.ds(256, 16), :].astype(F32)[0:1]
            k_rank = jnp.concatenate([k_rank] * 4, axis=1)
            shift = jnp.where(k_rank <= q_rank, lse, jnp.inf)
            parts.append(scores[i * 128:(i + 1) * 128] * (SCALE * LOG2E) - shift)
        exponent = jnp.concatenate(parts, axis=0)
        if kk == 0 and qc == 0:
            row = lax.broadcasted_iota(jnp.int32, (256, 512), 0) + kp * 256
            col = lax.broadcasted_iota(jnp.int32, (256, 512), 1)
            seen = (row <= col) | (row // 128 != col // 128)
            exponent = jnp.where(seen, exponent, -jnp.inf)
        probs = jnp.exp2(exponent)
        probs_b = probs.astype(BF)
        d_scores = (probs * (d_probs - delta)).astype(BF)
        rows = pl.ds(kp * 256, 256)
        d_v = dot(probs_b, do, NN)
        d_k = dot(d_scores, q, NN)
        d_q = dot(k_t[kk, :, rows], d_scores, NN)
        dv_acc[kk, rows, :] = d_v if first_k else dv_acc[kk, rows, :] + d_v
        dk_acc[kk, rows, :] = d_k if first_k else dk_acc[kk, rows, :] + d_k
        dq_acc[qc] = d_q if first_q else dq_acc[qc] + d_q

    step(1, 1, 0, True, True)
    step(1, 0, 0, True)
    for d in range(4):
        late_zp[d].wait_recv()
        go(late_fwd[d])
    step(0, 1, 0, True)
    step(0, 0, 0, True)
    for d in range(4):
        qa_sib[d].wait_recv()
        late_sib[d].wait_recv()
    step(1, 1, 1, False, True)
    step(1, 0, 1)
    step(1, 1, 2, False, True)
    step(1, 0, 2)
    for d in range(4):
        qa_fwd[d].wait_recv()
        late_fwd[d].wait_recv()
    kv_back = [remote(skv.at[d], rkv.at[d], across) for d in range(4)]
    for kp in (1, 0):
        step(1, kp, 3, False, kp == 1)
        for d in (2 * kp + 1, 2 * kp):
            rows = pl.ds(d * 128, 128)
            skv[d, pl.ds(0, 128), :] = dv_acc[1, rows, :].astype(BF)
            skv[d, pl.ds(128, 128), :] = (dk_acc[1, rows, :] * SCALE).astype(BF)
            go(kv_back[d])

    step(0, 1, 3)
    step(0, 0, 3)
    sq[0] = (dq_acc[3] * SCALE).astype(BF)
    q_back3 = remote(sq.at[0], rq.at[0], sibling)
    go(q_back3)
    step(0, 1, 2)
    step(0, 0, 2)
    q_back3.wait_recv()
    sq[1] = (dq_acc[2] * SCALE + rq[0].astype(F32)).astype(BF)
    q_back2 = remote(sq.at[1], rq.at[1], zpart)
    go(q_back2)
    step(0, 1, 1)
    step(0, 0, 1)
    sq[2] = (dq_acc[1] * SCALE).astype(BF)
    q_back1 = remote(sq.at[2], rq.at[2], sibling)
    go(q_back1)

    out_kv = [None] + [remote(fkv.at[d], out.at[m, pl.ds(128, 256)], from_z[d]) for d in (1, 2, 3)]
    out_q = [None] + [remote(fq.at[d], out.at[m, pl.ds(0, 128)], from_z[d]) for d in (1, 2, 3)]
    for d in (3, 2, 1, 0):
        rows = pl.ds(d * 128, 128)
        kv_back[d].wait_recv()
        fkv[d, pl.ds(0, 128), :] = (dv_acc[0, rows, :] + rkv[d, pl.ds(0, 128), :].astype(F32)).astype(BF)
        fkv[d, pl.ds(128, 128), :] = (
            dk_acc[0, rows, :] * SCALE + rkv[d, pl.ds(128, 128), :].astype(F32)
        ).astype(BF)
        if d > 0:
            go(out_kv[d])
    q_back1.wait_recv()
    q_back2.wait_recv()
    for d in (3, 2, 1, 0):
        rows = pl.ds(d * 128, 128)
        summed = dq_acc[0, :, rows] * SCALE + (rq[1, :, rows].astype(F32) + rq[2, :, rows].astype(F32))
        fq[d] = jnp.transpose(summed).astype(BF)
        if d > 0:
            go(out_q[d])
    out[m, pl.ds(128, 256), :] = fkv[0]
    out[m, pl.ds(0, 128), :] = fq[0]
    for d in (1, 2, 3):
        out_kv[d].wait_recv()
        out_q[d].wait_recv()
    for copy in started:
        copy.wait_send()


COPIES = 80


def on_device(queries, keys, values, outputs, lse, positions, w_out, d_layer):
    vmem = pl.BlockSpec(memory_space=pltpu.VMEM)
    hbm = pl.BlockSpec(memory_space=pl.ANY)
    grads = pl.pallas_call(
        kernel,
        out_shape=jax.ShapeDtypeStruct((4, 384, 128), BF),
        in_specs=[hbm] * 6 + [vmem] * 2,
        out_specs=vmem,
        scratch_shapes=[
            pltpu.VMEM((4, 128, 4, 128), BF),
            pltpu.VMEM((128, 512), BF),
            pltpu.VMEM((8, 128, 512), BF),
            pltpu.VMEM((8, 512, 512), BF),
            pltpu.VMEM((4, KV_ROWS, 128), BF),
            pltpu.VMEM((4, QA_ROWS, 128), BF),
            pltpu.VMEM((2, 4, KV_ROWS, 128), BF),
            pltpu.VMEM((4, 4, QA_ROWS, 128), BF),
            pltpu.VMEM((4, 4, QA_ROWS, 128), BF),
            pltpu.VMEM((4, QA_ROWS, 128), BF),
            pltpu.VMEM((2, 128, 512), BF),
            pltpu.VMEM((4, 128, 512), F32),
            pltpu.VMEM((2, 512, 128), F32),
            pltpu.VMEM((2, 512, 128), F32),
            pltpu.VMEM((3, 128, 512), BF),
            pltpu.VMEM((3, 128, 512), BF),
            pltpu.VMEM((4, 256, 128), BF),
            pltpu.VMEM((4, 256, 128), BF),
            pltpu.VMEM((4, 128, 128), BF),
            pltpu.VMEM((4, 256, 128), BF),
            pltpu.SemaphoreType.DMA((COPIES,)),
            pltpu.SemaphoreType.DMA((COPIES,)),
            pltpu.SemaphoreType.DMA((16,)),
        ],
        compiler_params=pltpu.CompilerParams(
            collective_id=0, has_side_effects=True, vmem_limit_bytes=VMEM_BYTES
        ),
    )(d_layer, w_out, values, keys, queries, outputs, lse, positions.reshape(1, 128))
    d_q, d_v, d_k = (jnp.transpose(grads[:, i * 128:(i + 1) * 128], (1, 0, 2)) for i in range(3))
    return (d_q, d_k, d_v)


def solution(mesh):
    in_specs = (
        P("blk", "head", None),
        P("blk", "head", None),
        P("blk", "head", None),
        P("blk", "head", None),
        P("head", "blk"),
        P("blk"),
        P("head", None),
        P("blk", "head"),
    )
    out_specs = (P("blk", "head", None), P("blk", "head", None), P("blk", "head", None))
    return jax.shard_map(
        on_device, mesh=mesh, in_specs=in_specs, out_specs=out_specs, check_vma=False
    )
```

```python
import functools
import math

import jax
import jax.numpy as jnp
from jax import lax
from jax.experimental import pallas as pl
from jax.experimental.pallas import tpu as pltpu
from jax.sharding import PartitionSpec as P

MESH = pl.DeviceIdType.MESH
BF = jnp.bfloat16
F32 = jnp.float32
LOG2E = 1.0 / math.log(2.0)
SCALE = 1.0 / math.sqrt(128.0)
KV_ROWS = 272
QA_ROWS = 144
VMEM_BYTES = 63 * 1024 * 1024
NT = (((1,), (1,)), ((), ()))
TN = (((0,), (0,)), ((), ()))
NN = (((1,), (0,)), ((), ()))


def dot(a, b, dims):
    return lax.dot_general(a, b, dims, preferred_element_type=F32)


def thirds(value):
    high = value.astype(BF)
    rest = value - high.astype(F32)
    middle = rest.astype(BF)
    low = (rest - middle.astype(F32)).astype(BF)
    return high, middle, low


def kernel(
    dl, w_hbm, v_hbm, k_hbm, q_hbm, o_hbm, lse_ref, pos_ref, out,
    raw, dl_v, gath, w_v, kv_st, qa_st, kv, qa, late, late_out, k_t, dq_acc, dk_acc, dv_acc,
    sq, rq, skv, rkv, fq, fkv, send, recv, local,
):
    b = lax.axis_index("blk")
    hd = lax.axis_index("head")
    yh, z, c = b // 16, (b // 2) % 8, b % 2
    m = z // 2
    sg = 2 * (z % 2) - 1
    x, yl = hd // 2, hd % 2

    def at_z(by):
        return {"blk": yh * 16 + ((z + by + 8) % 8) * 2 + c}

    sibling = {"blk": yh * 16 + z * 2 + (1 - c)}
    across = {"blk": (1 - yh) * 16 + z * 2 + c}
    zpart = at_z(-sg)
    to_z = (None, at_z(sg), at_z(-2 * sg), at_z(3 * sg))
    from_z = (None, at_z(sg), at_z(2 * sg), at_z(3 * sg))
    head_of = (m, (m + sg + 4) % 4, (m - sg + 4) % 4, (m + 2) % 4)
    beside = {"head": x * 2 + (1 - yl)}
    right = {"head": ((x + 1) % 4) * 2 + yl}
    left = {"head": ((x + 3) % 4) * 2 + yl}

    count = [0]
    started = []

    def remote(src, dst, device):
        k = count[0]
        count[0] = k + 1
        return pltpu.make_async_remote_copy(
            src_ref=src, dst_ref=dst, send_sem=send.at[k], recv_sem=recv.at[k],
            device_id=device, device_id_type=MESH,
        )

    def go(copy):
        copy.start()
        started.append(copy)

    raw_copies = [pltpu.make_async_copy(a, raw.at[i], local.at[8 + i]) for i, a in enumerate((v_hbm, k_hbm, q_hbm, o_hbm))]
    dl_copy = pltpu.make_async_copy(dl, dl_v, local.at[12])
    w_copies = []
    for r in range(8):
        dx, dy = r // 2, r % 2
        col = (((x + dx) % 4) * 2 + (yl + dy) % 2) * 512
        w_copies.append(
            pltpu.make_async_copy(w_hbm.at[:, pl.ds(pl.multiple_of(col, 512), 512)], w_v.at[r], local.at[r])
        )
    for copy in raw_copies[:3] + [dl_copy]:
        copy.start()

    barrier = pltpu.get_barrier_semaphore()
    partners = (beside, right, left, sibling, across, zpart, at_z(sg), at_z(-2 * sg), at_z(2 * sg), at_z(3 * sg))
    for device in partners:
        pl.semaphore_signal(barrier, inc=1, device_id=device, device_id_type=MESH)

    rank = jnp.broadcast_to((pos_ref[...] // 128).astype(F32)[:, 0:1], (1, 128))
    aux = []
    for h in range(4):
        parts = thirds(lse_ref[pl.ds(h, 1), :])
        rows = [rank] + [part.astype(F32) for part in parts] + [jnp.zeros((12, 128), F32)]
        aux.append(jnp.concatenate(rows, axis=0).astype(BF))

    def relay_out(i):
        raw_copies[i].wait()
        return jnp.transpose(raw[i].astype(F32), (1, 0, 2)).astype(BF)

    pl.semaphore_wait(barrier, len(partners))

    halves = (pl.ds(0, 64), pl.ds(64, 64))
    g_side = [remote(dl.at[r], gath.at[1, r], beside) for r in halves]
    g_r0 = [remote(dl.at[r], gath.at[6, r], right) for r in halves]
    g_l0 = [remote(dl.at[r], gath.at[2, r], left) for r in halves]
    g_r1 = [remote(gath.at[1, r], gath.at[7, r], right) for r in halves]
    g_l1 = [remote(gath.at[1, r], gath.at[3, r], left) for r in halves]
    g_r2 = remote(gath.at[6, halves[0]], gath.at[4, halves[0]], right)
    g_l2 = remote(gath.at[2, halves[1]], gath.at[4, halves[1]], left)
    g_r3 = remote(gath.at[7, halves[0]], gath.at[5, halves[0]], right)
    g_l3 = remote(gath.at[3, halves[1]], gath.at[5, halves[1]], left)
    for copy in (g_side[0], g_r0[0], g_l0[1], g_side[1], g_r0[1], g_l0[0]):
        go(copy)

    kv_st[:, pl.ds(0, 128), :] = relay_out(0)
    kv_st[:, pl.ds(128, 128), :] = relay_out(1)
    for h in range(4):
        kv_st[h, pl.ds(256, 16), :] = aux[h]
        qa_st[h, pl.ds(0, 16), :] = aux[h]
    kv_z = [None] + [remote(kv_st.at[head_of[d]], kv.at[0, d], to_z[d]) for d in (1, 2, 3)]
    qa_z = [None] + [remote(qa_st.at[head_of[d]], qa.at[0, d], to_z[d]) for d in (1, 2, 3)]
    qa_sib = [remote(qa_st.at[m] if d == 0 else qa.at[0, d], qa.at[1, d], sibling) for d in range(4)]
    qa_zp = [remote(qa_st.at[m] if d == 0 else qa.at[0, d], qa.at[2, d], zpart) for d in range(4)]
    qa_fwd = [remote(qa.at[2, d], qa.at[3, d], sibling) for d in range(4)]
    kv_y = [remote(kv_st.at[m] if d == 0 else kv.at[0, d], kv.at[1, d], across) for d in range(4)]
    for d in (3, 2, 1):
        go(kv_z[d])
    go(kv_y[0])
    for copy in (raw_copies[3], *(w_copies[r] for r in (0, 1, 6, 2, 7, 3, 4, 5))):
        copy.start()
    qa_st[:, pl.ds(16, 128), :] = relay_out(2)
    for d in (3, 2, 1):
        go(qa_z[d])
    go(qa_zp[0])
    go(qa_sib[0])
    kv[0, 0] = kv_st[m]
    qa[0, 0] = qa_st[m]

    def project(r):
        w_copies[r].wait()
        shard = dl_v[...] if r == 0 else gath[r]
        return dot(shard, w_v[r], NT)

    g_side[0].wait_recv()
    go(g_r1[0])
    go(g_l1[0])
    g_r0[0].wait_recv()
    go(g_r2)
    g_l0[1].wait_recv()
    go(g_l2)
    g_side[1].wait_recv()
    go(g_l1[1])
    go(g_r1[1])
    o_heads = relay_out(3)
    dl_copy.wait()
    total = project(0)
    total += project(1)
    g_r1[0].wait_recv()
    go(g_r3)
    g_l1[1].wait_recv()
    go(g_l3)
    g_r0[1].wait_recv()
    total += project(6)
    g_l0[0].wait_recv()
    total += project(2)
    g_r1[1].wait_recv()
    total += project(7)
    g_l1[0].wait_recv()
    total += project(3)
    for d in (1, 2, 3):
        kv_z[d].wait_recv()
        go(kv_y[d])
        qa_z[d].wait_recv()
        go(qa_zp[d])
        go(qa_sib[d])
    g_r2.wait_recv()
    g_l2.wait_recv()
    total += project(4)
    g_r3.wait_recv()
    g_l3.wait_recv()
    total += project(5)

    for h in range(4):
        part = total[:, h * 128:(h + 1) * 128].astype(BF)
        late_out[h, pl.ds(0, 128), :] = part
        col = jnp.sum(part.astype(F32) * o_heads[h].astype(F32), axis=1, keepdims=True)
        row = jnp.transpose(jnp.broadcast_to(col, (128, 128)))[0:1, :]
        rows = [part.astype(F32) for part in thirds(row)] + [jnp.zeros((13, 128), F32)]
        late_out[h, pl.ds(128, 16), :] = jnp.concatenate(rows, axis=0).astype(BF)

    late_z = [None] + [remote(late_out.at[head_of[d]], late.at[0, d], to_z[d]) for d in (1, 2, 3)]
    late_sib = [remote(late_out.at[m] if d == 0 else late.at[0, d], late.at[1, d], sibling) for d in range(4)]
    late_zp = [remote(late_out.at[m] if d == 0 else late.at[0, d], late.at[2, d], zpart) for d in range(4)]
    late_fwd = [remote(late.at[2, d], late.at[3, d], sibling) for d in range(4)]
    for d in (3, 2, 1):
        go(late_z[d])
    go(late_zp[0])
    go(late_sib[0])
    late[0, 0] = late_out[m]
    for d in range(4):
        qa_zp[d].wait_recv()
        go(qa_fwd[d])
    for d in range(4):
        k_t[0, :, pl.ds(d * 128, 128)] = jnp.transpose(kv[0, d, pl.ds(128, 128), :].astype(F32)).astype(BF)
    for d in range(4):
        kv_y[d].wait_recv()
        k_t[1, :, pl.ds(d * 128, 128)] = jnp.transpose(kv[1, d, pl.ds(128, 128), :].astype(F32)).astype(BF)
    for d in (1, 2, 3):
        late_z[d].wait_recv()
        go(late_zp[d])
        go(late_sib[d])

    def step(kk, kp, qc, first_k=False, first_q=False):
        keys = [kv[kk, 2 * kp + i, pl.ds(128, 128), :] for i in (0, 1)]
        k = jnp.concatenate(keys, axis=0)
        v = jnp.concatenate([kv[kk, 2 * kp + i, pl.ds(0, 128), :] for i in (0, 1)], axis=0)
        q = jnp.concatenate([qa[qc, i, pl.ds(16, 128), :] for i in range(4)], axis=0)
        do = jnp.concatenate([late[qc, i, pl.ds(0, 128), :] for i in range(4)], axis=0)
        aux = jnp.concatenate([qa[qc, i, pl.ds(0, 16), :].astype(F32) for i in range(4)], axis=1)
        aux2 = jnp.concatenate([late[qc, i, pl.ds(128, 16), :].astype(F32) for i in range(4)], axis=1)
        q_rank = aux[0:1]
        lse = (aux[1:2] + aux[2:3] + aux[3:4]) * LOG2E
        delta = aux2[0:1] + aux2[1:2] + aux2[2:3]
        scores = dot(k, q, NT)
        d_probs = dot(v, do, NT)
        parts = []
        for i in (0, 1):
            k_rank = kv[kk, 2 * kp + i, pl.ds(256, 16), :].astype(F32)[0:1]
            k_rank = jnp.concatenate([k_rank] * 4, axis=1)
            shift = jnp.where(k_rank <= q_rank, lse, jnp.inf)
            parts.append(scores[i * 128:(i + 1) * 128] * (SCALE * LOG2E) - shift)
        exponent = jnp.concatenate(parts, axis=0)
        if kk == 0 and qc == 0:
            row = lax.broadcasted_iota(jnp.int32, (256, 512), 0) + kp * 256
            col = lax.broadcasted_iota(jnp.int32, (256, 512), 1)
            seen = (row <= col) | (row // 128 != col // 128)
            exponent = jnp.where(seen, exponent, -jnp.inf)
        probs = jnp.exp2(exponent)
        probs_b = probs.astype(BF)
        d_scores = (probs * (d_probs - delta)).astype(BF)
        rows = pl.ds(kp * 256, 256)
        d_v = dot(probs_b, do, NN)
        d_k = dot(d_scores, q, NN)
        d_q = dot(k_t[kk, :, rows], d_scores, NN)
        dv_acc[kk, rows, :] = d_v if first_k else dv_acc[kk, rows, :] + d_v
        dk_acc[kk, rows, :] = d_k if first_k else dk_acc[kk, rows, :] + d_k
        dq_acc[qc] = d_q if first_q else dq_acc[qc] + d_q

    step(1, 1, 0, True, True)
    step(1, 0, 0, True)
    for d in range(4):
        late_zp[d].wait_recv()
        go(late_fwd[d])
    step(0, 1, 0, True)
    step(0, 0, 0, True)
    for d in range(4):
        qa_sib[d].wait_recv()
        late_sib[d].wait_recv()
    step(1, 1, 1, False, True)
    step(1, 0, 1)
    step(1, 1, 2, False, True)
    step(1, 0, 2)
    for d in range(4):
        qa_fwd[d].wait_recv()
        late_fwd[d].wait_recv()
    kv_back = [remote(skv.at[d], rkv.at[d], across) for d in range(4)]
    for kp in (1, 0):
        step(1, kp, 3, False, kp == 1)
        for d in (2 * kp + 1, 2 * kp):
            rows = pl.ds(d * 128, 128)
            skv[d, pl.ds(0, 128), :] = dv_acc[1, rows, :].astype(BF)
            skv[d, pl.ds(128, 128), :] = (dk_acc[1, rows, :] * SCALE).astype(BF)
            go(kv_back[d])

    step(0, 1, 3)
    step(0, 0, 3)
    sq[0] = (dq_acc[3] * SCALE).astype(BF)
    q_back3 = remote(sq.at[0], rq.at[0], sibling)
    go(q_back3)
    step(0, 1, 2)
    step(0, 0, 2)
    q_back3.wait_recv()
    sq[1] = (dq_acc[2] * SCALE + rq[0].astype(F32)).astype(BF)
    q_back2 = remote(sq.at[1], rq.at[1], zpart)
    go(q_back2)
    step(0, 1, 1)
    step(0, 0, 1)
    sq[2] = (dq_acc[1] * SCALE).astype(BF)
    q_back1 = remote(sq.at[2], rq.at[2], sibling)
    go(q_back1)

    out_kv = [None] + [remote(fkv.at[d], out.at[m, pl.ds(128, 256)], from_z[d]) for d in (1, 2, 3)]
    out_q = [None] + [remote(fq.at[d], out.at[m, pl.ds(0, 128)], from_z[d]) for d in (1, 2, 3)]
    for d in (3, 2, 1, 0):
        rows = pl.ds(d * 128, 128)
        kv_back[d].wait_recv()
        fkv[d, pl.ds(0, 128), :] = (dv_acc[0, rows, :] + rkv[d, pl.ds(0, 128), :].astype(F32)).astype(BF)
        fkv[d, pl.ds(128, 128), :] = (
            dk_acc[0, rows, :] * SCALE + rkv[d, pl.ds(128, 128), :].astype(F32)
        ).astype(BF)
        if d > 0:
            go(out_kv[d])
    keep_kv = pltpu.make_async_copy(fkv.at[0], out.at[m, pl.ds(128, 256)], local.at[14])
    keep_kv.start()
    q_back1.wait_recv()
    q_back2.wait_recv()
    for d in (3, 2, 1, 0):
        rows = pl.ds(d * 128, 128)
        summed = dq_acc[0, :, rows] * SCALE + (rq[1, :, rows].astype(F32) + rq[2, :, rows].astype(F32))
        fq[d] = jnp.transpose(summed).astype(BF)
        if d > 0:
            go(out_q[d])
    keep_q = pltpu.make_async_copy(fq.at[0], out.at[m, pl.ds(0, 128)], local.at[13])
    keep_q.start()
    keep_kv.wait()
    keep_q.wait()
    for d in (1, 2, 3):
        out_kv[d].wait_recv()
        out_q[d].wait_recv()
    for copy in started:
        copy.wait_send()


COPIES = 80


def token_major(blocks, d_q, d_k, d_v, held, turned, sem):
    outs = ((0, d_q), (2, d_k), (1, d_v))
    loads = [pltpu.make_async_copy(blocks.at[:, pl.ds(128 * i, 128)], held.at[i], sem.at[i]) for i, _ in outs]
    stores = [pltpu.make_async_copy(turned.at[i], out, sem.at[3 + i]) for i, out in outs]
    for load in loads:
        load.start()
    for (i, _), load, store in zip(outs, loads, stores):
        load.wait()
        turned[i] = jnp.transpose(held[i].astype(F32), (1, 0, 2)).astype(BF)
        store.start()
    for store in stores:
        store.wait()


def on_device(queries, keys, values, outputs, lse, positions, w_out, d_layer):
    vmem = pl.BlockSpec(memory_space=pltpu.VMEM)
    hbm = pl.BlockSpec(memory_space=pl.ANY)
    grads = pl.pallas_call(
        kernel,
        out_shape=jax.ShapeDtypeStruct((4, 384, 128), BF),
        in_specs=[hbm] * 6 + [vmem] * 2,
        out_specs=hbm,
        scratch_shapes=[
            pltpu.VMEM((4, 128, 4, 128), BF),
            pltpu.VMEM((128, 512), BF),
            pltpu.VMEM((8, 128, 512), BF),
            pltpu.VMEM((8, 512, 512), BF),
            pltpu.VMEM((4, KV_ROWS, 128), BF),
            pltpu.VMEM((4, QA_ROWS, 128), BF),
            pltpu.VMEM((2, 4, KV_ROWS, 128), BF),
            pltpu.VMEM((4, 4, QA_ROWS, 128), BF),
            pltpu.VMEM((4, 4, QA_ROWS, 128), BF),
            pltpu.VMEM((4, QA_ROWS, 128), BF),
            pltpu.VMEM((2, 128, 512), BF),
            pltpu.VMEM((4, 128, 512), F32),
            pltpu.VMEM((2, 512, 128), F32),
            pltpu.VMEM((2, 512, 128), F32),
            pltpu.VMEM((3, 128, 512), BF),
            pltpu.VMEM((3, 128, 512), BF),
            pltpu.VMEM((4, 256, 128), BF),
            pltpu.VMEM((4, 256, 128), BF),
            pltpu.VMEM((4, 128, 128), BF),
            pltpu.VMEM((4, 256, 128), BF),
            pltpu.SemaphoreType.DMA((COPIES,)),
            pltpu.SemaphoreType.DMA((COPIES,)),
            pltpu.SemaphoreType.DMA((16,)),
        ],
        compiler_params=pltpu.CompilerParams(
            collective_id=0, has_side_effects=True, vmem_limit_bytes=VMEM_BYTES
        ),
    )(d_layer, w_out, values, keys, queries, outputs, lse, positions.reshape(1, 128))
    return pl.pallas_call(
        token_major,
        out_shape=[jax.ShapeDtypeStruct((128, 4, 128), BF)] * 3,
        in_specs=[hbm],
        out_specs=[hbm] * 3,
        scratch_shapes=[
            pltpu.VMEM((3, 4, 128, 128), BF),
            pltpu.VMEM((3, 128, 4, 128), BF),
            pltpu.SemaphoreType.DMA((6,)),
        ],
        compiler_params=pltpu.CompilerParams(vmem_limit_bytes=VMEM_BYTES),
    )(grads)


def solution(mesh):
    in_specs = (
        P("blk", "head", None),
        P("blk", "head", None),
        P("blk", "head", None),
        P("blk", "head", None),
        P("head", "blk"),
        P("blk"),
        P("head", None),
        P("blk", "head"),
    )
    out_specs = (P("blk", "head", None), P("blk", "head", None), P("blk", "head", None))
    return jax.shard_map(
        on_device, mesh=mesh, in_specs=in_specs, out_specs=out_specs, check_vma=False
    )
```

```python
import functools
import math

import jax
import jax.numpy as jnp
from jax import lax
from jax.experimental import pallas as pl
from jax.experimental.pallas import tpu as pltpu
from jax.sharding import PartitionSpec as P

MESH = pl.DeviceIdType.MESH
BF = jnp.bfloat16
F32 = jnp.float32
LOG2E = 1.0 / math.log(2.0)
SCALE = 1.0 / math.sqrt(128.0)
KV_ROWS = 272
QA_ROWS = 144
VMEM_BYTES = 63 * 1024 * 1024
NT = (((1,), (1,)), ((), ()))
TN = (((0,), (0,)), ((), ()))
NN = (((1,), (0,)), ((), ()))


def dot(a, b, dims):
    return lax.dot_general(a, b, dims, preferred_element_type=F32)


def thirds(value):
    high = value.astype(BF)
    rest = value - high.astype(F32)
    middle = rest.astype(BF)
    low = (rest - middle.astype(F32)).astype(BF)
    return high, middle, low


def kernel(
    dl, w_hbm, v_hbm, k_hbm, q_hbm, o_hbm, lse_ref, pos_ref, out,
    raw, dl_v, gath, w_v, kv_st, qa_st, kv, qa, late, late_out, k_t, dq_acc, dk_acc, dv_acc,
    sq, rq, skv, rkv, fq, fkv, send, recv, local,
):
    b = lax.axis_index("blk")
    hd = lax.axis_index("head")
    yh, z, c = b // 16, (b // 2) % 8, b % 2
    m = z // 2
    sg = 2 * (z % 2) - 1
    x, yl = hd // 2, hd % 2

    def at_z(by):
        return {"blk": yh * 16 + ((z + by + 8) % 8) * 2 + c}

    sibling = {"blk": yh * 16 + z * 2 + (1 - c)}
    across = {"blk": (1 - yh) * 16 + z * 2 + c}
    zpart = at_z(-sg)
    to_z = (None, at_z(sg), at_z(-2 * sg), at_z(3 * sg))
    from_z = (None, at_z(sg), at_z(2 * sg), at_z(3 * sg))
    head_of = (m, (m + sg + 4) % 4, (m - sg + 4) % 4, (m + 2) % 4)
    beside = {"head": x * 2 + (1 - yl)}
    right = {"head": ((x + 1) % 4) * 2 + yl}
    left = {"head": ((x + 3) % 4) * 2 + yl}

    count = [0]
    started = []

    def remote(src, dst, device):
        k = count[0]
        count[0] = k + 1
        return pltpu.make_async_remote_copy(
            src_ref=src, dst_ref=dst, send_sem=send.at[k], recv_sem=recv.at[k],
            device_id=device, device_id_type=MESH,
        )

    def go(copy):
        copy.start()
        started.append(copy)

    raw_copies = [pltpu.make_async_copy(a, raw.at[i], local.at[8 + i]) for i, a in enumerate((v_hbm, k_hbm, q_hbm, o_hbm))]
    dl_copy = pltpu.make_async_copy(dl, dl_v, local.at[12])
    w_copies = []
    for r in range(8):
        dx, dy = r // 2, r % 2
        col = (((x + dx) % 4) * 2 + (yl + dy) % 2) * 512
        w_copies.append(
            pltpu.make_async_copy(w_hbm.at[:, pl.ds(pl.multiple_of(col, 512), 512)], w_v.at[r], local.at[r])
        )
    for copy in [raw_copies[i] for i in (2, 0, 1)] + [dl_copy, raw_copies[3]] + [w_copies[r] for r in (0, 1, 6, 2, 7, 3, 4, 5)]:
        copy.start()

    barrier = pltpu.get_barrier_semaphore()
    partners = (beside, right, left, sibling, across, zpart, at_z(sg), at_z(-2 * sg), at_z(2 * sg), at_z(3 * sg))
    for device in partners:
        pl.semaphore_signal(barrier, inc=1, device_id=device, device_id_type=MESH)

    rank = jnp.broadcast_to((pos_ref[...] // 128).astype(F32)[:, 0:1], (1, 128))
    aux = []
    for h in range(4):
        parts = thirds(lse_ref[pl.ds(h, 1), :])
        rows = [rank] + [part.astype(F32) for part in parts] + [jnp.zeros((12, 128), F32)]
        aux.append(jnp.concatenate(rows, axis=0).astype(BF))

    def relay_out(i):
        raw_copies[i].wait()
        return jnp.transpose(raw[i].astype(F32), (1, 0, 2)).astype(BF)

    pl.semaphore_wait(barrier, len(partners))

    halves = (pl.ds(0, 64), pl.ds(64, 64))
    g_side = [remote(dl.at[r], gath.at[1, r], beside) for r in halves]
    g_r0 = [remote(dl.at[r], gath.at[6, r], right) for r in halves]
    g_l0 = [remote(dl.at[r], gath.at[2, r], left) for r in halves]
    g_r1 = [remote(gath.at[1, r], gath.at[7, r], right) for r in halves]
    g_l1 = [remote(gath.at[1, r], gath.at[3, r], left) for r in halves]
    g_r2 = remote(gath.at[6, halves[0]], gath.at[4, halves[0]], right)
    g_l2 = remote(gath.at[2, halves[1]], gath.at[4, halves[1]], left)
    g_r3 = remote(gath.at[7, halves[0]], gath.at[5, halves[0]], right)
    g_l3 = remote(gath.at[3, halves[1]], gath.at[5, halves[1]], left)
    for copy in (g_side[0], g_r0[0], g_l0[1], g_side[1], g_r0[1], g_l0[0]):
        go(copy)

    kv_z = [None] + [remote(kv_st.at[head_of[d]], kv.at[0, d], to_z[d]) for d in (1, 2, 3)]
    qa_z = [None] + [remote(qa_st.at[head_of[d]], qa.at[0, d], to_z[d]) for d in (1, 2, 3)]
    qa_sib = [remote(qa_st.at[m] if d == 0 else qa.at[0, d], qa.at[1, d], sibling) for d in range(4)]
    qa_zp = [remote(qa_st.at[m] if d == 0 else qa.at[0, d], qa.at[2, d], zpart) for d in range(4)]
    qa_fwd = [remote(qa.at[2, d], qa.at[3, d], sibling) for d in range(4)]
    kv_y = [remote(kv_st.at[m] if d == 0 else kv.at[0, d], kv.at[1, d], across) for d in range(4)]
    qa_st[:, pl.ds(16, 128), :] = relay_out(2)
    for h in range(4):
        kv_st[h, pl.ds(256, 16), :] = aux[h]
        qa_st[h, pl.ds(0, 16), :] = aux[h]
    for d in (3, 2, 1):
        go(qa_z[d])
    go(qa_zp[0])
    go(qa_sib[0])
    kv_st[:, pl.ds(0, 128), :] = relay_out(0)
    kv_st[:, pl.ds(128, 128), :] = relay_out(1)
    for d in (3, 2, 1):
        go(kv_z[d])
    go(kv_y[0])
    kv[0, 0] = kv_st[m]
    qa[0, 0] = qa_st[m]

    def project(r):
        w_copies[r].wait()
        shard = dl_v[...] if r == 0 else gath[r]
        return dot(shard, w_v[r], NT)

    def pass_keys(d):
        kv_z[d].wait_recv()
        go(kv_y[d])

    def pass_queries(d):
        qa_z[d].wait_recv()
        go(qa_zp[d])
        go(qa_sib[d])

    g_side[0].wait_recv()
    go(g_r1[0])
    go(g_l1[0])
    g_r0[0].wait_recv()
    go(g_r2)
    g_l0[1].wait_recv()
    go(g_l2)
    g_side[1].wait_recv()
    go(g_l1[1])
    go(g_r1[1])
    o_heads = relay_out(3)
    dl_copy.wait()
    total = project(0)
    total += project(1)
    pass_queries(3)
    g_r1[0].wait_recv()
    go(g_r3)
    g_l1[1].wait_recv()
    go(g_l3)
    pass_queries(2)
    g_r0[1].wait_recv()
    total += project(6)
    g_l0[0].wait_recv()
    total += project(2)
    pass_queries(1)
    g_r1[1].wait_recv()
    total += project(7)
    g_l1[0].wait_recv()
    total += project(3)
    pass_keys(3)
    g_r2.wait_recv()
    g_l2.wait_recv()
    total += project(4)
    pass_keys(2)
    g_r3.wait_recv()
    g_l3.wait_recv()
    total += project(5)

    for h in range(4):
        part = total[:, h * 128:(h + 1) * 128].astype(BF)
        late_out[h, pl.ds(0, 128), :] = part
        col = jnp.sum(part.astype(F32) * o_heads[h].astype(F32), axis=1, keepdims=True)
        row = jnp.transpose(jnp.broadcast_to(col, (128, 128)))[0:1, :]
        rows = [part.astype(F32) for part in thirds(row)] + [jnp.zeros((13, 128), F32)]
        late_out[h, pl.ds(128, 16), :] = jnp.concatenate(rows, axis=0).astype(BF)

    late_z = [None] + [remote(late_out.at[head_of[d]], late.at[0, d], to_z[d]) for d in (1, 2, 3)]
    late_sib = [remote(late_out.at[m] if d == 0 else late.at[0, d], late.at[1, d], sibling) for d in range(4)]
    late_zp = [remote(late_out.at[m] if d == 0 else late.at[0, d], late.at[2, d], zpart) for d in range(4)]
    late_fwd = [remote(late.at[2, d], late.at[3, d], sibling) for d in range(4)]
    for d in (3, 2, 1):
        go(late_z[d])
    go(late_zp[0])
    go(late_sib[0])
    late[0, 0] = late_out[m]
    pass_keys(1)
    for d in (0, 3, 2, 1):
        qa_zp[d].wait_recv()
        go(qa_fwd[d])
    for d in (3, 2, 1):
        late_z[d].wait_recv()
        go(late_zp[d])
        go(late_sib[d])
    for d in range(4):
        k_t[0, :, pl.ds(d * 128, 128)] = jnp.transpose(kv[0, d, pl.ds(128, 128), :].astype(F32)).astype(BF)
    for d in range(4):
        kv_y[d].wait_recv()
        k_t[1, :, pl.ds(d * 128, 128)] = jnp.transpose(kv[1, d, pl.ds(128, 128), :].astype(F32)).astype(BF)

    def step(kk, kp, qc, first_k=False, first_q=False):
        keys = [kv[kk, 2 * kp + i, pl.ds(128, 128), :] for i in (0, 1)]
        k = jnp.concatenate(keys, axis=0)
        v = jnp.concatenate([kv[kk, 2 * kp + i, pl.ds(0, 128), :] for i in (0, 1)], axis=0)
        q = jnp.concatenate([qa[qc, i, pl.ds(16, 128), :] for i in range(4)], axis=0)
        do = jnp.concatenate([late[qc, i, pl.ds(0, 128), :] for i in range(4)], axis=0)
        aux = jnp.concatenate([qa[qc, i, pl.ds(0, 16), :].astype(F32) for i in range(4)], axis=1)
        aux2 = jnp.concatenate([late[qc, i, pl.ds(128, 16), :].astype(F32) for i in range(4)], axis=1)
        q_rank = aux[0:1]
        lse = (aux[1:2] + aux[2:3] + aux[3:4]) * LOG2E
        delta = aux2[0:1] + aux2[1:2] + aux2[2:3]
        scores = dot(k, q, NT)
        d_probs = dot(v, do, NT)
        parts = []
        for i in (0, 1):
            k_rank = kv[kk, 2 * kp + i, pl.ds(256, 16), :].astype(F32)[0:1]
            k_rank = jnp.concatenate([k_rank] * 4, axis=1)
            shift = jnp.where(k_rank <= q_rank, lse, jnp.inf)
            parts.append(scores[i * 128:(i + 1) * 128] * (SCALE * LOG2E) - shift)
        exponent = jnp.concatenate(parts, axis=0)
        if kk == 0 and qc == 0:
            row = lax.broadcasted_iota(jnp.int32, (256, 512), 0) + kp * 256
            col = lax.broadcasted_iota(jnp.int32, (256, 512), 1)
            seen = (row <= col) | (row // 128 != col // 128)
            exponent = jnp.where(seen, exponent, -jnp.inf)
        probs = jnp.exp2(exponent)
        probs_b = probs.astype(BF)
        d_scores = (probs * (d_probs - delta)).astype(BF)
        rows = pl.ds(kp * 256, 256)
        d_v = dot(probs_b, do, NN)
        d_k = dot(d_scores, q, NN)
        d_q = dot(k_t[kk, :, rows], d_scores, NN)
        dv_acc[kk, rows, :] = d_v if first_k else dv_acc[kk, rows, :] + d_v
        dk_acc[kk, rows, :] = d_k if first_k else dk_acc[kk, rows, :] + d_k
        dq_acc[qc] = d_q if first_q else dq_acc[qc] + d_q

    step(1, 1, 0, True, True)
    step(1, 0, 0, True)
    for d in (0, 3, 2, 1):
        late_zp[d].wait_recv()
        go(late_fwd[d])
    step(0, 1, 0, True)
    step(0, 0, 0, True)
    for d in range(4):
        qa_sib[d].wait_recv()
        late_sib[d].wait_recv()
    step(1, 1, 1, False, True)
    step(1, 0, 1)
    step(1, 1, 2, False, True)
    step(1, 0, 2)
    for d in range(4):
        qa_fwd[d].wait_recv()
        late_fwd[d].wait_recv()
    kv_back = [remote(skv.at[d], rkv.at[d], across) for d in range(4)]
    for kp in (1, 0):
        step(1, kp, 3, False, kp == 1)
        for d in (2 * kp + 1, 2 * kp):
            rows = pl.ds(d * 128, 128)
            skv[d, pl.ds(0, 128), :] = dv_acc[1, rows, :].astype(BF)
            skv[d, pl.ds(128, 128), :] = (dk_acc[1, rows, :] * SCALE).astype(BF)
            go(kv_back[d])

    step(0, 1, 3)
    step(0, 0, 3)
    sq[0] = (dq_acc[3] * SCALE).astype(BF)
    q_back3 = remote(sq.at[0], rq.at[0], sibling)
    go(q_back3)
    step(0, 1, 2)
    step(0, 0, 2)
    q_back3.wait_recv()
    q_back2 = [None] * 4
    for d in (3, 2, 1, 0):
        cols = pl.ds(d * 128, 128)
        sq[1, :, cols] = (dq_acc[2, :, cols] * SCALE + rq[0, :, cols].astype(F32)).astype(BF)
        q_back2[d] = remote(sq.at[1, :, cols], rq.at[1, :, cols], zpart)
        go(q_back2[d])
    step(0, 1, 1)
    step(0, 0, 1)
    sq[2] = (dq_acc[1] * SCALE).astype(BF)
    q_back1 = remote(sq.at[2], rq.at[2], sibling)
    go(q_back1)

    out_kv = [None] + [remote(fkv.at[d], out.at[m, pl.ds(128, 256)], from_z[d]) for d in (1, 2, 3)]
    out_q = [None] + [remote(fq.at[d], out.at[m, pl.ds(0, 128)], from_z[d]) for d in (1, 2, 3)]
    for d in (3, 2, 1, 0):
        rows = pl.ds(d * 128, 128)
        kv_back[d].wait_recv()
        fkv[d, pl.ds(0, 128), :] = (dv_acc[0, rows, :] + rkv[d, pl.ds(0, 128), :].astype(F32)).astype(BF)
        fkv[d, pl.ds(128, 128), :] = (
            dk_acc[0, rows, :] * SCALE + rkv[d, pl.ds(128, 128), :].astype(F32)
        ).astype(BF)
        if d > 0:
            go(out_kv[d])
    keep_kv = pltpu.make_async_copy(fkv.at[0], out.at[m, pl.ds(128, 256)], local.at[14])
    keep_kv.start()
    q_back1.wait_recv()
    for d in (3, 2, 1, 0):
        rows = pl.ds(d * 128, 128)
        q_back2[d].wait_recv()
        summed = dq_acc[0, :, rows] * SCALE + (rq[1, :, rows].astype(F32) + rq[2, :, rows].astype(F32))
        fq[d] = jnp.transpose(summed).astype(BF)
        if d > 0:
            go(out_q[d])
    keep_q = pltpu.make_async_copy(fq.at[0], out.at[m, pl.ds(0, 128)], local.at[13])
    keep_q.start()
    for copy in started:
        copy.wait_send()
    for d in (1, 2, 3):
        out_kv[d].wait_recv()
        out_q[d].wait_recv()
    keep_kv.wait()
    keep_q.wait()


COPIES = 80


def token_major(blocks, d_q, d_k, d_v, held, turned, sem):
    outs = ((0, d_q), (2, d_k), (1, d_v))
    loads = [pltpu.make_async_copy(blocks.at[:, pl.ds(128 * i, 128)], held.at[i], sem.at[i]) for i, _ in outs]
    stores = [pltpu.make_async_copy(turned.at[i], out, sem.at[3 + i]) for i, out in outs]
    for load in loads:
        load.start()
    for (i, _), load, store in zip(outs, loads, stores):
        load.wait()
        turned[i] = jnp.transpose(held[i].astype(F32), (1, 0, 2)).astype(BF)
        store.start()
    for store in stores:
        store.wait()


def on_device(queries, keys, values, outputs, lse, positions, w_out, d_layer):
    vmem = pl.BlockSpec(memory_space=pltpu.VMEM)
    hbm = pl.BlockSpec(memory_space=pl.ANY)
    grads = pl.pallas_call(
        kernel,
        out_shape=jax.ShapeDtypeStruct((4, 384, 128), BF),
        in_specs=[hbm] * 6 + [vmem] * 2,
        out_specs=hbm,
        scratch_shapes=[
            pltpu.VMEM((4, 128, 4, 128), BF),
            pltpu.VMEM((128, 512), BF),
            pltpu.VMEM((8, 128, 512), BF),
            pltpu.VMEM((8, 512, 512), BF),
            pltpu.VMEM((4, KV_ROWS, 128), BF),
            pltpu.VMEM((4, QA_ROWS, 128), BF),
            pltpu.VMEM((2, 4, KV_ROWS, 128), BF),
            pltpu.VMEM((4, 4, QA_ROWS, 128), BF),
            pltpu.VMEM((4, 4, QA_ROWS, 128), BF),
            pltpu.VMEM((4, QA_ROWS, 128), BF),
            pltpu.VMEM((2, 128, 512), BF),
            pltpu.VMEM((4, 128, 512), F32),
            pltpu.VMEM((2, 512, 128), F32),
            pltpu.VMEM((2, 512, 128), F32),
            pltpu.VMEM((3, 128, 512), BF),
            pltpu.VMEM((3, 128, 512), BF),
            pltpu.VMEM((4, 256, 128), BF),
            pltpu.VMEM((4, 256, 128), BF),
            pltpu.VMEM((4, 128, 128), BF),
            pltpu.VMEM((4, 256, 128), BF),
            pltpu.SemaphoreType.DMA((COPIES,)),
            pltpu.SemaphoreType.DMA((COPIES,)),
            pltpu.SemaphoreType.DMA((16,)),
        ],
        compiler_params=pltpu.CompilerParams(
            collective_id=0, has_side_effects=True, vmem_limit_bytes=VMEM_BYTES
        ),
    )(d_layer, w_out, values, keys, queries, outputs, lse, positions.reshape(1, 128))
    return pl.pallas_call(
        token_major,
        out_shape=[jax.ShapeDtypeStruct((128, 4, 128), BF)] * 3,
        in_specs=[hbm],
        out_specs=[hbm] * 3,
        scratch_shapes=[
            pltpu.VMEM((3, 4, 128, 128), BF),
            pltpu.VMEM((3, 128, 4, 128), BF),
            pltpu.SemaphoreType.DMA((6,)),
        ],
        compiler_params=pltpu.CompilerParams(vmem_limit_bytes=VMEM_BYTES),
    )(grads)


def solution(mesh):
    in_specs = (
        P("blk", "head", None),
        P("blk", "head", None),
        P("blk", "head", None),
        P("blk", "head", None),
        P("head", "blk"),
        P("blk"),
        P("head", None),
        P("blk", "head"),
    )
    out_specs = (P("blk", "head", None), P("blk", "head", None), P("blk", "head", None))
    return jax.shard_map(
        on_device, mesh=mesh, in_specs=in_specs, out_specs=out_specs, check_vma=False
    )
```

```python
import functools
import math

import jax
import jax.numpy as jnp
from jax import lax
from jax.experimental import pallas as pl
from jax.experimental.pallas import tpu as pltpu
from jax.sharding import PartitionSpec as P

MESH = pl.DeviceIdType.MESH
BF = jnp.bfloat16
F32 = jnp.float32
LOG2E = 1.0 / math.log(2.0)
SCALE = 1.0 / math.sqrt(128.0)
KV_ROWS = 272
QA_ROWS = 144
VMEM_BYTES = 63 * 1024 * 1024
NT = (((1,), (1,)), ((), ()))
TN = (((0,), (0,)), ((), ()))
NN = (((1,), (0,)), ((), ()))


def dot(a, b, dims):
    return lax.dot_general(a, b, dims, preferred_element_type=F32)


def thirds(value):
    high = value.astype(BF)
    rest = value - high.astype(F32)
    middle = rest.astype(BF)
    low = (rest - middle.astype(F32)).astype(BF)
    return high, middle, low


def kernel(
    dl, w_hbm, v_hbm, k_hbm, q_hbm, o_hbm, lse_ref, pos_ref, out,
    raw, dl_v, gath, w_v, kv_st, qa_st, kv, qa, late, late_out, k_t, dq_acc, dk_acc, dv_acc,
    sq, rq, skv, rkv, fq, fkv, send, recv, local,
):
    b = lax.axis_index("blk")
    hd = lax.axis_index("head")
    yh, z, c = b // 16, (b // 2) % 8, b % 2
    m = z // 2
    sg = 2 * (z % 2) - 1
    x, yl = hd // 2, hd % 2

    def at_z(by):
        return {"blk": yh * 16 + ((z + by + 8) % 8) * 2 + c}

    sibling = {"blk": yh * 16 + z * 2 + (1 - c)}
    across = {"blk": (1 - yh) * 16 + z * 2 + c}
    zpart = at_z(-sg)
    to_z = (None, at_z(sg), at_z(-2 * sg), at_z(3 * sg))
    from_z = (None, at_z(sg), at_z(2 * sg), at_z(3 * sg))
    head_of = (m, (m + sg + 4) % 4, (m - sg + 4) % 4, (m + 2) % 4)
    beside = {"head": x * 2 + (1 - yl)}
    right = {"head": ((x + 1) % 4) * 2 + yl}
    left = {"head": ((x + 3) % 4) * 2 + yl}

    count = [0]
    started = []

    def remote(src, dst, device):
        k = count[0]
        count[0] = k + 1
        return pltpu.make_async_remote_copy(
            src_ref=src, dst_ref=dst, send_sem=send.at[k], recv_sem=recv.at[k],
            device_id=device, device_id_type=MESH,
        )

    def go(copy):
        copy.start()
        started.append(copy)

    raw_copies = [pltpu.make_async_copy(a, raw.at[i], local.at[8 + i]) for i, a in enumerate((v_hbm, k_hbm, q_hbm, o_hbm))]
    dl_copy = pltpu.make_async_copy(dl, dl_v, local.at[12])
    w_copies = []
    for r in range(8):
        dx, dy = r // 2, r % 2
        col = (((x + dx) % 4) * 2 + (yl + dy) % 2) * 512
        w_copies.append(
            pltpu.make_async_copy(w_hbm.at[:, pl.ds(pl.multiple_of(col, 512), 512)], w_v.at[r], local.at[r])
        )
    for copy in [raw_copies[i] for i in (2, 0, 1)] + [dl_copy, raw_copies[3]] + [w_copies[r] for r in (0, 1, 4, 6, 2, 7, 3, 5)]:
        copy.start()

    barrier = pltpu.get_barrier_semaphore()
    partners = (beside, right, left, sibling, across, zpart, at_z(sg), at_z(-2 * sg), at_z(2 * sg), at_z(3 * sg))
    for device in partners:
        pl.semaphore_signal(barrier, inc=1, device_id=device, device_id_type=MESH)

    rank = jnp.broadcast_to((pos_ref[...] // 128).astype(F32)[:, 0:1], (1, 128))
    aux = []
    for h in range(4):
        parts = thirds(lse_ref[pl.ds(h, 1), :])
        rows = [rank] + [part.astype(F32) for part in parts] + [jnp.zeros((12, 128), F32)]
        aux.append(jnp.concatenate(rows, axis=0).astype(BF))

    def relay_out(i):
        raw_copies[i].wait()
        return jnp.transpose(raw[i], (1, 0, 2))

    pl.semaphore_wait(barrier, len(partners))

    halves = (pl.ds(0, 64), pl.ds(64, 64))
    g_side = [remote(dl.at[r], gath.at[1, r], beside) for r in halves]
    g_r0 = [remote(dl.at[r], gath.at[6, r], right) for r in halves]
    g_l0 = [remote(dl.at[r], gath.at[2, r], left) for r in halves]
    g_r1 = [remote(gath.at[1, r], gath.at[7, r], right) for r in halves]
    g_l1 = [remote(gath.at[1, r], gath.at[3, r], left) for r in halves]
    g_r2 = remote(gath.at[6, halves[0]], gath.at[4, halves[0]], right)
    g_l2 = remote(gath.at[2, halves[1]], gath.at[4, halves[1]], left)
    g_far = [remote(gath.at[4, r], gath.at[5, r], beside) for r in halves]
    for copy in (g_side[0], g_r0[0], g_l0[1], g_side[1], g_r0[1], g_l0[0]):
        go(copy)

    kv_z = [None] + [remote(kv_st.at[head_of[d]], kv.at[0, d], to_z[d]) for d in (1, 2, 3)]
    qa_z = [None] + [remote(qa_st.at[head_of[d]], qa.at[0, d], to_z[d]) for d in (1, 2, 3)]
    qa_sib = [remote(qa_st.at[m] if d == 0 else qa.at[0, d], qa.at[1, d], sibling) for d in range(4)]
    qa_zp = [remote(qa_st.at[m] if d == 0 else qa.at[0, d], qa.at[2, d], zpart) for d in range(4)]
    qa_fwd = [remote(qa.at[2, d], qa.at[3, d], sibling) for d in range(4)]
    kv_y = [remote(kv_st.at[m] if d == 0 else kv.at[0, d], kv.at[1, d], across) for d in range(4)]
    qa_st[:, pl.ds(16, 128), :] = relay_out(2)
    for h in range(4):
        kv_st[h, pl.ds(256, 16), :] = aux[h]
        qa_st[h, pl.ds(0, 16), :] = aux[h]
    for d in (3, 2, 1):
        go(qa_z[d])
    go(qa_zp[0])
    go(qa_sib[0])
    kv_st[:, pl.ds(0, 128), :] = relay_out(0)
    kv_st[:, pl.ds(128, 128), :] = relay_out(1)
    for d in (3, 2, 1):
        go(kv_z[d])
    kv[0, 0] = kv_st[m]
    qa[0, 0] = qa_st[m]

    def project(r):
        w_copies[r].wait()
        shard = dl_v[...] if r == 0 else gath[r]
        return dot(shard, w_v[r], NT)

    def pass_keys(d):
        kv_z[d].wait_recv()
        go(kv_y[d])

    def pass_queries(d):
        qa_z[d].wait_recv()
        go(qa_zp[d])
        go(qa_sib[d])

    g_r0[0].wait_recv()
    go(g_r2)
    g_l0[1].wait_recv()
    go(g_l2)
    g_side[0].wait_recv()
    go(g_r1[0])
    go(g_l1[0])
    g_side[1].wait_recv()
    go(g_l1[1])
    go(g_r1[1])
    o_heads = relay_out(3)
    dl_copy.wait()
    total = project(0)
    total += project(1)
    pass_queries(3)
    g_r2.wait_recv()
    go(g_far[0])
    g_l2.wait_recv()
    go(g_far[1])
    pass_queries(2)
    go(kv_y[0])
    total += project(4)
    g_r0[1].wait_recv()
    total += project(6)
    g_l0[0].wait_recv()
    total += project(2)
    pass_queries(1)
    for f in (0, 1):
        g_r1[f].wait_recv()
        g_l1[f].wait_recv()
    total += project(7)
    total += project(3)
    pass_keys(3)
    g_far[0].wait_recv()
    g_far[1].wait_recv()
    total += project(5)
    pass_keys(2)

    for h in range(4):
        part = total[:, h * 128:(h + 1) * 128].astype(BF)
        late_out[h, pl.ds(0, 128), :] = part
        col = jnp.sum(part.astype(F32) * o_heads[h].astype(F32), axis=1, keepdims=True)
        row = jnp.transpose(jnp.broadcast_to(col, (128, 128)))[0:1, :]
        rows = [part.astype(F32) for part in thirds(row)] + [jnp.zeros((13, 128), F32)]
        late_out[h, pl.ds(128, 16), :] = jnp.concatenate(rows, axis=0).astype(BF)

    late_z = [None] + [remote(late_out.at[head_of[d]], late.at[0, d], to_z[d]) for d in (1, 2, 3)]
    late_sib = [remote(late_out.at[m] if d == 0 else late.at[0, d], late.at[1, d], sibling) for d in range(4)]
    late_zp = [remote(late_out.at[m] if d == 0 else late.at[0, d], late.at[2, d], zpart) for d in range(4)]
    late_fwd = [remote(late.at[2, d], late.at[3, d], sibling) for d in range(4)]
    for d in (3, 2, 1):
        go(late_z[d])
    go(late_zp[0])
    go(late_sib[0])
    late[0, 0] = late_out[m]
    pass_keys(1)
    for d in (0, 3, 2, 1):
        qa_zp[d].wait_recv()
        go(qa_fwd[d])
    def turn_across(d):
        kv_y[d].wait_recv()
        k_t[1, :, pl.ds(d * 128, 128)] = jnp.transpose(kv[1, d, pl.ds(128, 128), :].astype(F32)).astype(BF)

    for d in range(4):
        k_t[0, :, pl.ds(d * 128, 128)] = jnp.transpose(kv[0, d, pl.ds(128, 128), :].astype(F32)).astype(BF)
    for d in (0, 3, 2):
        turn_across(d)
    for d in (3, 2, 1):
        late_z[d].wait_recv()
        go(late_zp[d])
        go(late_sib[d])
    turn_across(1)

    def step(kk, kp, qc, first_k=False, first_q=False):
        keys = [kv[kk, 2 * kp + i, pl.ds(128, 128), :] for i in (0, 1)]
        k = jnp.concatenate(keys, axis=0)
        v = jnp.concatenate([kv[kk, 2 * kp + i, pl.ds(0, 128), :] for i in (0, 1)], axis=0)
        q = jnp.concatenate([qa[qc, i, pl.ds(16, 128), :] for i in range(4)], axis=0)
        do = jnp.concatenate([late[qc, i, pl.ds(0, 128), :] for i in range(4)], axis=0)
        aux = jnp.concatenate([qa[qc, i, pl.ds(0, 16), :].astype(F32) for i in range(4)], axis=1)
        aux2 = jnp.concatenate([late[qc, i, pl.ds(128, 16), :].astype(F32) for i in range(4)], axis=1)
        q_rank = aux[0:1]
        lse = (aux[1:2] + aux[2:3] + aux[3:4]) * LOG2E
        delta = aux2[0:1] + aux2[1:2] + aux2[2:3]
        scores = dot(k, q, NT)
        d_probs = dot(v, do, NT)
        parts = []
        for i in (0, 1):
            k_rank = kv[kk, 2 * kp + i, pl.ds(256, 16), :].astype(F32)[0:1]
            k_rank = jnp.concatenate([k_rank] * 4, axis=1)
            shift = jnp.where(k_rank <= q_rank, lse, jnp.inf)
            parts.append(scores[i * 128:(i + 1) * 128] * (SCALE * LOG2E) - shift)
        exponent = jnp.concatenate(parts, axis=0)
        if kk == 0 and qc == 0:
            row = lax.broadcasted_iota(jnp.int32, (256, 512), 0) + kp * 256
            col = lax.broadcasted_iota(jnp.int32, (256, 512), 1)
            seen = (row <= col) | (row // 128 != col // 128)
            exponent = jnp.where(seen, exponent, -jnp.inf)
        probs = jnp.exp2(exponent)
        probs_b = probs.astype(BF)
        d_scores = (probs * (d_probs - delta)).astype(BF)
        rows = pl.ds(kp * 256, 256)
        d_v = dot(probs_b, do, NN)
        d_k = dot(d_scores, q, NN)
        d_q = dot(k_t[kk, :, rows], d_scores, NN)
        dv_acc[kk, rows, :] = d_v if first_k else dv_acc[kk, rows, :] + d_v
        dk_acc[kk, rows, :] = d_k if first_k else dk_acc[kk, rows, :] + d_k
        dq_acc[qc] = d_q if first_q else dq_acc[qc] + d_q

    step(1, 1, 0, True, True)
    step(1, 0, 0, True)
    for d in (0, 3, 2, 1):
        late_zp[d].wait_recv()
        go(late_fwd[d])
    for d in range(4):
        qa_sib[d].wait_recv()
        late_sib[d].wait_recv()
    step(1, 1, 1, False, True)
    step(1, 0, 1)
    step(1, 1, 2, False, True)
    step(1, 0, 2)
    for d in range(4):
        qa_fwd[d].wait_recv()
        late_fwd[d].wait_recv()
    kv_back = [remote(skv.at[d], rkv.at[d], across) for d in range(4)]
    for kp in (1, 0):
        step(1, kp, 3, False, kp == 1)
        for d in (2 * kp + 1, 2 * kp):
            rows = pl.ds(d * 128, 128)
            skv[d, pl.ds(0, 128), :] = dv_acc[1, rows, :].astype(BF)
            skv[d, pl.ds(128, 128), :] = (dk_acc[1, rows, :] * SCALE).astype(BF)
            go(kv_back[d])

    step(0, 1, 3, True)
    step(0, 0, 3, True)
    sq[0] = (dq_acc[3] * SCALE).astype(BF)
    q_back3 = remote(sq.at[0], rq.at[0], sibling)
    go(q_back3)
    step(0, 1, 2)
    step(0, 0, 2)
    q_back3.wait_recv()
    q_back2 = [None] * 4
    for d in (3, 2, 1, 0):
        cols = pl.ds(d * 128, 128)
        sq[1, :, cols] = (dq_acc[2, :, cols] * SCALE + rq[0, :, cols].astype(F32)).astype(BF)
        q_back2[d] = remote(sq.at[1, :, cols], rq.at[1, :, cols], zpart)
        go(q_back2[d])
    step(0, 1, 1)
    step(0, 0, 1)
    sq[2] = (dq_acc[1] * SCALE).astype(BF)
    q_back1 = remote(sq.at[2], rq.at[2], sibling)
    go(q_back1)
    step(0, 1, 0)
    step(0, 0, 0)

    out_kv = [None] + [remote(fkv.at[d], out.at[m, pl.ds(128, 256)], from_z[d]) for d in (1, 2, 3)]
    out_q = [None] + [remote(fq.at[d], out.at[m, pl.ds(0, 128)], from_z[d]) for d in (1, 2, 3)]
    for d in (3, 2, 1, 0):
        rows = pl.ds(d * 128, 128)
        kv_back[d].wait_recv()
        fkv[d, pl.ds(0, 128), :] = (dv_acc[0, rows, :] + rkv[d, pl.ds(0, 128), :].astype(F32)).astype(BF)
        fkv[d, pl.ds(128, 128), :] = (
            dk_acc[0, rows, :] * SCALE + rkv[d, pl.ds(128, 128), :].astype(F32)
        ).astype(BF)
        if d > 0:
            go(out_kv[d])
    keep_kv = pltpu.make_async_copy(fkv.at[0], out.at[m, pl.ds(128, 256)], local.at[14])
    keep_kv.start()
    q_back1.wait_recv()
    for d in (3, 2, 1, 0):
        rows = pl.ds(d * 128, 128)
        q_back2[d].wait_recv()
        summed = dq_acc[0, :, rows] * SCALE + (rq[1, :, rows].astype(F32) + rq[2, :, rows].astype(F32))
        fq[d] = jnp.transpose(summed).astype(BF)
        if d > 0:
            go(out_q[d])
    keep_q = pltpu.make_async_copy(fq.at[0], out.at[m, pl.ds(0, 128)], local.at[13])
    keep_q.start()
    for copy in started:
        copy.wait_send()
    for d in (1, 2, 3):
        out_kv[d].wait_recv()
        out_q[d].wait_recv()
    keep_kv.wait()
    keep_q.wait()


COPIES = 80


def token_major(blocks, d_q, d_k, d_v, held, turned, sem):
    outs = ((0, d_q), (2, d_k), (1, d_v))
    loads = [pltpu.make_async_copy(blocks.at[:, pl.ds(128 * i, 128)], held.at[i], sem.at[i]) for i, _ in outs]
    stores = [pltpu.make_async_copy(turned.at[i], out, sem.at[3 + i]) for i, out in outs]
    for load in loads:
        load.start()
    for (i, _), load, store in zip(outs, loads, stores):
        load.wait()
        turned[i] = jnp.transpose(held[i], (1, 0, 2))
        store.start()
    for store in stores:
        store.wait()


def on_device(queries, keys, values, outputs, lse, positions, w_out, d_layer):
    vmem = pl.BlockSpec(memory_space=pltpu.VMEM)
    hbm = pl.BlockSpec(memory_space=pl.ANY)
    grads = pl.pallas_call(
        kernel,
        out_shape=jax.ShapeDtypeStruct((4, 384, 128), BF),
        in_specs=[hbm] * 6 + [vmem] * 2,
        out_specs=hbm,
        scratch_shapes=[
            pltpu.VMEM((4, 128, 4, 128), BF),
            pltpu.VMEM((128, 512), BF),
            pltpu.VMEM((8, 128, 512), BF),
            pltpu.VMEM((8, 512, 512), BF),
            pltpu.VMEM((4, KV_ROWS, 128), BF),
            pltpu.VMEM((4, QA_ROWS, 128), BF),
            pltpu.VMEM((2, 4, KV_ROWS, 128), BF),
            pltpu.VMEM((4, 4, QA_ROWS, 128), BF),
            pltpu.VMEM((4, 4, QA_ROWS, 128), BF),
            pltpu.VMEM((4, QA_ROWS, 128), BF),
            pltpu.VMEM((2, 128, 512), BF),
            pltpu.VMEM((4, 128, 512), F32),
            pltpu.VMEM((2, 512, 128), F32),
            pltpu.VMEM((2, 512, 128), F32),
            pltpu.VMEM((3, 128, 512), BF),
            pltpu.VMEM((3, 128, 512), BF),
            pltpu.VMEM((4, 256, 128), BF),
            pltpu.VMEM((4, 256, 128), BF),
            pltpu.VMEM((4, 128, 128), BF),
            pltpu.VMEM((4, 256, 128), BF),
            pltpu.SemaphoreType.DMA((COPIES,)),
            pltpu.SemaphoreType.DMA((COPIES,)),
            pltpu.SemaphoreType.DMA((16,)),
        ],
        compiler_params=pltpu.CompilerParams(
            collective_id=0, has_side_effects=True, vmem_limit_bytes=VMEM_BYTES
        ),
    )(d_layer, w_out, values, keys, queries, outputs, lse, positions.reshape(1, 128))
    return pl.pallas_call(
        token_major,
        out_shape=[jax.ShapeDtypeStruct((128, 4, 128), BF)] * 3,
        in_specs=[hbm],
        out_specs=[hbm] * 3,
        scratch_shapes=[
            pltpu.VMEM((3, 4, 128, 128), BF),
            pltpu.VMEM((3, 128, 4, 128), BF),
            pltpu.SemaphoreType.DMA((6,)),
        ],
        compiler_params=pltpu.CompilerParams(vmem_limit_bytes=VMEM_BYTES),
    )(grads)


def solution(mesh):
    in_specs = (
        P("blk", "head", None),
        P("blk", "head", None),
        P("blk", "head", None),
        P("blk", "head", None),
        P("head", "blk"),
        P("blk"),
        P("head", None),
        P("blk", "head"),
    )
    out_specs = (P("blk", "head", None), P("blk", "head", None), P("blk", "head", None))
    return jax.shard_map(
        on_device, mesh=mesh, in_specs=in_specs, out_specs=out_specs, check_vma=False
    )
```

```python
import functools
import math

import jax
import jax.numpy as jnp
from jax import lax
from jax.experimental import pallas as pl
from jax.experimental.pallas import tpu as pltpu
from jax.sharding import PartitionSpec as P

MESH = pl.DeviceIdType.MESH
BF = jnp.bfloat16
F32 = jnp.float32
LOG2E = 1.0 / math.log(2.0)
SCALE = 1.0 / math.sqrt(128.0)
KV_ROWS = 272
QA_ROWS = 144
VMEM_BYTES = 63 * 1024 * 1024
NT = (((1,), (1,)), ((), ()))
TN = (((0,), (0,)), ((), ()))
NN = (((1,), (0,)), ((), ()))


def dot(a, b, dims):
    return lax.dot_general(a, b, dims, preferred_element_type=F32)


def thirds(value):
    high = value.astype(BF)
    rest = value - high.astype(F32)
    middle = rest.astype(BF)
    low = (rest - middle.astype(F32)).astype(BF)
    return high, middle, low


def kernel(
    dl, w_hbm, v_hbm, k_hbm, q_hbm, o_hbm, lse_ref, pos_ref, out,
    raw, dl_v, gath, w_v, kv_st, qa_st, kv, qa, late, late_out, k_t, dq_acc, dk_acc, dv_acc,
    sq, rq, skv, rkv, fq, fkv, send, recv, local,
):
    b = lax.axis_index("blk")
    hd = lax.axis_index("head")
    yh, z, c = b // 16, (b // 2) % 8, b % 2
    m = z // 2
    sg = 2 * (z % 2) - 1
    x, yl = hd // 2, hd % 2

    def at_z(by):
        return {"blk": yh * 16 + ((z + by + 8) % 8) * 2 + c}

    sibling = {"blk": yh * 16 + z * 2 + (1 - c)}
    across = {"blk": (1 - yh) * 16 + z * 2 + c}
    zpart = at_z(-sg)
    to_z = (None, at_z(sg), at_z(-2 * sg), at_z(3 * sg))
    from_z = (None, at_z(sg), at_z(2 * sg), at_z(3 * sg))
    head_of = (m, (m + sg + 4) % 4, (m - sg + 4) % 4, (m + 2) % 4)
    beside = {"head": x * 2 + (1 - yl)}
    right = {"head": ((x + 1) % 4) * 2 + yl}
    left = {"head": ((x + 3) % 4) * 2 + yl}

    count = [0]
    started = []

    def remote(src, dst, device):
        k = count[0]
        count[0] = k + 1
        return pltpu.make_async_remote_copy(
            src_ref=src, dst_ref=dst, send_sem=send.at[k], recv_sem=recv.at[k],
            device_id=device, device_id_type=MESH,
        )

    def go(copy):
        copy.start()
        started.append(copy)

    raw_copies = [pltpu.make_async_copy(a, raw.at[i], local.at[8 + i]) for i, a in enumerate((v_hbm, k_hbm, q_hbm, o_hbm))]
    dl_copy = pltpu.make_async_copy(dl, dl_v, local.at[12])
    w_copies = []
    for r in range(8):
        dx, dy = r // 2, r % 2
        col = (((x + dx) % 4) * 2 + (yl + dy) % 2) * 512
        w_copies.append(
            pltpu.make_async_copy(w_hbm.at[:, pl.ds(pl.multiple_of(col, 512), 512)], w_v.at[r], local.at[r])
        )
    for copy in [raw_copies[i] for i in (2, 0, 1)] + [dl_copy, raw_copies[3]] + [w_copies[r] for r in (0, 1, 6, 2, 7, 3, 4, 5)]:
        copy.start()

    barrier = pltpu.get_barrier_semaphore()
    partners = (beside, right, left, sibling, across, zpart, at_z(sg), at_z(-2 * sg), at_z(2 * sg), at_z(3 * sg))
    for device in partners:
        pl.semaphore_signal(barrier, inc=1, device_id=device, device_id_type=MESH)

    rank = jnp.broadcast_to((pos_ref[...] // 128).astype(F32)[:, 0:1], (1, 128))
    aux = []
    for h in range(4):
        parts = thirds(lse_ref[pl.ds(h, 1), :])
        rows = [rank] + [part.astype(F32) for part in parts] + [jnp.zeros((12, 128), F32)]
        aux.append(jnp.concatenate(rows, axis=0).astype(BF))

    def relay_out(i):
        raw_copies[i].wait()
        return jnp.transpose(raw[i], (1, 0, 2))

    pl.semaphore_wait(barrier, len(partners))

    halves = (pl.ds(0, 64), pl.ds(64, 64))
    g_side = [remote(dl.at[r], gath.at[1, r], beside) for r in halves]
    g_r0 = [remote(dl.at[r], gath.at[6, r], right) for r in halves]
    g_l0 = [remote(dl.at[r], gath.at[2, r], left) for r in halves]
    g_r1 = [remote(gath.at[1, r], gath.at[7, r], right) for r in halves]
    g_l1 = [remote(gath.at[1, r], gath.at[3, r], left) for r in halves]
    g_r2 = remote(gath.at[6, halves[0]], gath.at[4, halves[0]], right)
    g_l2 = remote(gath.at[2, halves[1]], gath.at[4, halves[1]], left)
    g_r3 = remote(gath.at[7, halves[0]], gath.at[5, halves[0]], right)
    g_l3 = remote(gath.at[3, halves[1]], gath.at[5, halves[1]], left)
    for copy in (g_side[0], g_r0[0], g_l0[1], g_side[1], g_r0[1], g_l0[0]):
        go(copy)

    kv_z = [None] + [remote(kv_st.at[head_of[d]], kv.at[0, d], to_z[d]) for d in (1, 2, 3)]
    qa_z = [None] + [remote(qa_st.at[head_of[d]], qa.at[0, d], to_z[d]) for d in (1, 2, 3)]
    qa_sib = [remote(qa_st.at[m] if d == 0 else qa.at[0, d], qa.at[1, d], sibling) for d in range(4)]
    qa_zp = [remote(qa_st.at[m] if d == 0 else qa.at[0, d], qa.at[2, d], zpart) for d in range(4)]
    qa_fwd = [remote(qa.at[2, d], qa.at[3, d], sibling) for d in range(4)]
    kv_y = [remote(kv_st.at[m] if d == 0 else kv.at[0, d], kv.at[1, d], across) for d in range(4)]
    qa_st[:, pl.ds(16, 128), :] = relay_out(2)
    for h in range(4):
        kv_st[h, pl.ds(256, 16), :] = aux[h]
        qa_st[h, pl.ds(0, 16), :] = aux[h]
    for d in (3, 2, 1):
        go(qa_z[d])
    go(qa_zp[0])
    go(qa_sib[0])
    kv_st[:, pl.ds(0, 128), :] = relay_out(0)
    kv_st[:, pl.ds(128, 128), :] = relay_out(1)
    for d in (3, 2, 1):
        go(kv_z[d])
    go(kv_y[0])
    kv[0, 0] = kv_st[m]
    qa[0, 0] = qa_st[m]

    def project(r):
        w_copies[r].wait()
        shard = dl_v[...] if r == 0 else gath[r]
        return dot(shard, w_v[r], NT)

    def pass_keys(d):
        kv_z[d].wait_recv()
        go(kv_y[d])

    def pass_queries(d):
        qa_z[d].wait_recv()
        go(qa_zp[d])
        go(qa_sib[d])

    g_side[0].wait_recv()
    go(g_r1[0])
    go(g_l1[0])
    g_r0[0].wait_recv()
    go(g_r2)
    g_l0[1].wait_recv()
    go(g_l2)
    g_side[1].wait_recv()
    go(g_l1[1])
    go(g_r1[1])
    o_heads = relay_out(3)
    dl_copy.wait()
    total = project(0)
    total += project(1)
    pass_queries(3)
    g_r1[0].wait_recv()
    go(g_r3)
    g_l1[1].wait_recv()
    go(g_l3)
    pass_queries(2)
    g_r0[1].wait_recv()
    total += project(6)
    g_l0[0].wait_recv()
    total += project(2)
    pass_queries(1)
    g_r1[1].wait_recv()
    total += project(7)
    g_l1[0].wait_recv()
    total += project(3)
    pass_keys(3)
    g_r2.wait_recv()
    g_l2.wait_recv()
    total += project(4)
    pass_keys(2)
    g_r3.wait_recv()
    g_l3.wait_recv()
    total += project(5)

    for h in range(4):
        part = total[:, h * 128:(h + 1) * 128].astype(BF)
        late_out[h, pl.ds(0, 128), :] = part
        col = jnp.sum(part.astype(F32) * o_heads[h].astype(F32), axis=1, keepdims=True)
        row = jnp.transpose(jnp.broadcast_to(col, (128, 128)))[0:1, :]
        rows = [part.astype(F32) for part in thirds(row)] + [jnp.zeros((13, 128), F32)]
        late_out[h, pl.ds(128, 16), :] = jnp.concatenate(rows, axis=0).astype(BF)

    late_z = [None] + [remote(late_out.at[head_of[d]], late.at[0, d], to_z[d]) for d in (1, 2, 3)]
    late_sib = [remote(late_out.at[m] if d == 0 else late.at[0, d], late.at[1, d], sibling) for d in range(4)]
    late_zp = [remote(late_out.at[m] if d == 0 else late.at[0, d], late.at[2, d], zpart) for d in range(4)]
    late_fwd = [remote(late.at[2, d], late.at[3, d], sibling) for d in range(4)]
    for d in (3, 2, 1):
        go(late_z[d])
    go(late_zp[0])
    go(late_sib[0])
    late[0, 0] = late_out[m]
    pass_keys(1)
    for d in (0, 3, 2, 1):
        qa_zp[d].wait_recv()
        go(qa_fwd[d])
    def turn_across(d):
        kv_y[d].wait_recv()
        k_t[1, :, pl.ds(d * 128, 128)] = jnp.transpose(kv[1, d, pl.ds(128, 128), :].astype(F32)).astype(BF)

    for d in range(4):
        k_t[0, :, pl.ds(d * 128, 128)] = jnp.transpose(kv[0, d, pl.ds(128, 128), :].astype(F32)).astype(BF)
    for d in (0, 3, 2):
        turn_across(d)
    for d in (3, 2, 1):
        late_z[d].wait_recv()
        go(late_zp[d])
        go(late_sib[d])
    turn_across(1)

    def step(kk, kp, qc, first_k=False, first_q=False):
        keys = [kv[kk, 2 * kp + i, pl.ds(128, 128), :] for i in (0, 1)]
        k = jnp.concatenate(keys, axis=0)
        v = jnp.concatenate([kv[kk, 2 * kp + i, pl.ds(0, 128), :] for i in (0, 1)], axis=0)
        q = jnp.concatenate([qa[qc, i, pl.ds(16, 128), :] for i in range(4)], axis=0)
        do = jnp.concatenate([late[qc, i, pl.ds(0, 128), :] for i in range(4)], axis=0)
        aux = jnp.concatenate([qa[qc, i, pl.ds(0, 16), :].astype(F32) for i in range(4)], axis=1)
        aux2 = jnp.concatenate([late[qc, i, pl.ds(128, 16), :].astype(F32) for i in range(4)], axis=1)
        q_rank = aux[0:1]
        lse = (aux[1:2] + aux[2:3] + aux[3:4]) * LOG2E
        delta = aux2[0:1] + aux2[1:2] + aux2[2:3]
        scores = dot(k, q, NT)
        d_probs = dot(v, do, NT)
        parts = []
        for i in (0, 1):
            k_rank = kv[kk, 2 * kp + i, pl.ds(256, 16), :].astype(F32)[0:1]
            k_rank = jnp.concatenate([k_rank] * 4, axis=1)
            shift = jnp.where(k_rank <= q_rank, lse, jnp.inf)
            parts.append(scores[i * 128:(i + 1) * 128] * (SCALE * LOG2E) - shift)
        exponent = jnp.concatenate(parts, axis=0)
        if kk == 0 and qc == 0:
            row = lax.broadcasted_iota(jnp.int32, (256, 512), 0) + kp * 256
            col = lax.broadcasted_iota(jnp.int32, (256, 512), 1)
            seen = (row <= col) | (row // 128 != col // 128)
            exponent = jnp.where(seen, exponent, -jnp.inf)
        probs = jnp.exp2(exponent)
        probs_b = probs.astype(BF)
        d_scores = (probs * (d_probs - delta)).astype(BF)
        rows = pl.ds(kp * 256, 256)
        d_v = dot(probs_b, do, NN)
        d_k = dot(d_scores, q, NN)
        d_q = dot(k_t[kk, :, rows], d_scores, NN)
        dv_acc[kk, rows, :] = d_v if first_k else dv_acc[kk, rows, :] + d_v
        dk_acc[kk, rows, :] = d_k if first_k else dk_acc[kk, rows, :] + d_k
        dq_acc[qc] = d_q if first_q else dq_acc[qc] + d_q

    step(1, 1, 0, True, True)
    step(1, 0, 0, True)
    for d in (0, 3, 2, 1):
        late_zp[d].wait_recv()
        go(late_fwd[d])
    for d in range(4):
        qa_sib[d].wait_recv()
        late_sib[d].wait_recv()
    step(1, 1, 1, False, True)
    step(1, 0, 1)
    step(1, 1, 2, False, True)
    step(1, 0, 2)
    for d in range(4):
        qa_fwd[d].wait_recv()
        late_fwd[d].wait_recv()
    kv_back = [remote(skv.at[d], rkv.at[d], across) for d in range(4)]
    for kp in (1, 0):
        step(1, kp, 3, False, kp == 1)
        for d in (2 * kp + 1, 2 * kp):
            rows = pl.ds(d * 128, 128)
            skv[d, pl.ds(0, 128), :] = dv_acc[1, rows, :].astype(BF)
            skv[d, pl.ds(128, 128), :] = (dk_acc[1, rows, :] * SCALE).astype(BF)
            go(kv_back[d])

    step(0, 1, 3, True)
    step(0, 0, 3, True)
    sq[0] = (dq_acc[3] * SCALE).astype(BF)
    q_back3 = remote(sq.at[0], rq.at[0], sibling)
    go(q_back3)
    step(0, 1, 2)
    step(0, 0, 2)
    q_back3.wait_recv()
    q_back2 = [None] * 4
    for d in (3, 2, 1, 0):
        cols = pl.ds(d * 128, 128)
        sq[1, :, cols] = (dq_acc[2, :, cols] * SCALE + rq[0, :, cols].astype(F32)).astype(BF)
        q_back2[d] = remote(sq.at[1, :, cols], rq.at[1, :, cols], zpart)
        go(q_back2[d])
    step(0, 1, 1)
    step(0, 0, 1)
    sq[2] = (dq_acc[1] * SCALE).astype(BF)
    q_back1 = remote(sq.at[2], rq.at[2], sibling)
    go(q_back1)
    step(0, 1, 0)
    step(0, 0, 0)

    out_kv = [None] + [remote(fkv.at[d], out.at[m, pl.ds(128, 256)], from_z[d]) for d in (1, 2, 3)]
    out_q = [None] + [remote(fq.at[d], out.at[m, pl.ds(0, 128)], from_z[d]) for d in (1, 2, 3)]
    for d in (3, 2, 1, 0):
        rows = pl.ds(d * 128, 128)
        kv_back[d].wait_recv()
        fkv[d, pl.ds(0, 128), :] = (dv_acc[0, rows, :] + rkv[d, pl.ds(0, 128), :].astype(F32)).astype(BF)
        fkv[d, pl.ds(128, 128), :] = (
            dk_acc[0, rows, :] * SCALE + rkv[d, pl.ds(128, 128), :].astype(F32)
        ).astype(BF)
        if d > 0:
            go(out_kv[d])
    keep_kv = pltpu.make_async_copy(fkv.at[0], out.at[m, pl.ds(128, 256)], local.at[14])
    keep_kv.start()
    q_back1.wait_recv()
    for d in (3, 2, 1, 0):
        rows = pl.ds(d * 128, 128)
        q_back2[d].wait_recv()
        summed = dq_acc[0, :, rows] * SCALE + (rq[1, :, rows].astype(F32) + rq[2, :, rows].astype(F32))
        fq[d] = jnp.transpose(summed).astype(BF)
        if d > 0:
            go(out_q[d])
    keep_q = pltpu.make_async_copy(fq.at[0], out.at[m, pl.ds(0, 128)], local.at[13])
    keep_q.start()
    for copy in started:
        copy.wait_send()
    for d in (1, 2, 3):
        out_kv[d].wait_recv()
        out_q[d].wait_recv()
    keep_kv.wait()
    keep_q.wait()


COPIES = 80


def token_major(blocks, d_q, d_k, d_v, held, turned, sem):
    outs = ((0, d_q), (2, d_k), (1, d_v))
    loads = [pltpu.make_async_copy(blocks.at[:, pl.ds(128 * i, 128)], held.at[i], sem.at[i]) for i, _ in outs]
    stores = [pltpu.make_async_copy(turned.at[i], out, sem.at[3 + i]) for i, out in outs]
    for load in loads:
        load.start()
    for (i, _), load, store in zip(outs, loads, stores):
        load.wait()
        turned[i] = jnp.transpose(held[i], (1, 0, 2))
        store.start()
    for store in stores:
        store.wait()


def on_device(queries, keys, values, outputs, lse, positions, w_out, d_layer):
    vmem = pl.BlockSpec(memory_space=pltpu.VMEM)
    hbm = pl.BlockSpec(memory_space=pl.ANY)
    grads = pl.pallas_call(
        kernel,
        out_shape=jax.ShapeDtypeStruct((4, 384, 128), BF),
        in_specs=[hbm] * 6 + [vmem] * 2,
        out_specs=hbm,
        scratch_shapes=[
            pltpu.VMEM((4, 128, 4, 128), BF),
            pltpu.VMEM((128, 512), BF),
            pltpu.VMEM((8, 128, 512), BF),
            pltpu.VMEM((8, 512, 512), BF),
            pltpu.VMEM((4, KV_ROWS, 128), BF),
            pltpu.VMEM((4, QA_ROWS, 128), BF),
            pltpu.VMEM((2, 4, KV_ROWS, 128), BF),
            pltpu.VMEM((4, 4, QA_ROWS, 128), BF),
            pltpu.VMEM((4, 4, QA_ROWS, 128), BF),
            pltpu.VMEM((4, QA_ROWS, 128), BF),
            pltpu.VMEM((2, 128, 512), BF),
            pltpu.VMEM((4, 128, 512), F32),
            pltpu.VMEM((2, 512, 128), F32),
            pltpu.VMEM((2, 512, 128), F32),
            pltpu.VMEM((3, 128, 512), BF),
            pltpu.VMEM((3, 128, 512), BF),
            pltpu.VMEM((4, 256, 128), BF),
            pltpu.VMEM((4, 256, 128), BF),
            pltpu.VMEM((4, 128, 128), BF),
            pltpu.VMEM((4, 256, 128), BF),
            pltpu.SemaphoreType.DMA((COPIES,)),
            pltpu.SemaphoreType.DMA((COPIES,)),
            pltpu.SemaphoreType.DMA((16,)),
        ],
        compiler_params=pltpu.CompilerParams(
            collective_id=0, has_side_effects=True, vmem_limit_bytes=VMEM_BYTES
        ),
    )(d_layer, w_out, values, keys, queries, outputs, lse, positions.reshape(1, 128))
    return pl.pallas_call(
        token_major,
        out_shape=[jax.ShapeDtypeStruct((128, 4, 128), BF)] * 3,
        in_specs=[hbm],
        out_specs=[hbm] * 3,
        scratch_shapes=[
            pltpu.VMEM((3, 4, 128, 128), BF),
            pltpu.VMEM((3, 128, 4, 128), BF),
            pltpu.SemaphoreType.DMA((6,)),
        ],
        compiler_params=pltpu.CompilerParams(vmem_limit_bytes=VMEM_BYTES),
    )(grads)


def solution(mesh):
    in_specs = (
        P("blk", "head", None),
        P("blk", "head", None),
        P("blk", "head", None),
        P("blk", "head", None),
        P("head", "blk"),
        P("blk"),
        P("head", None),
        P("blk", "head"),
    )
    out_specs = (P("blk", "head", None), P("blk", "head", None), P("blk", "head", None))
    return jax.shard_map(
        on_device, mesh=mesh, in_specs=in_specs, out_specs=out_specs, check_vma=False
    )
```
